512 devices in a mesh: rows: 64 (over y, z), cols: 8 (over x, core).
Axes of the slice: x: 4, y: 4, z: 16, core: 2. Of those that a mesh axis runs over, the one named last changes fastest.
Arguments:
- descriptors: bfloat16 [16384, 1024], P(('rows', 'cols')), may hold values from -6 to 6
- sparse_points: bfloat16 [8192, 1024], P('cols'), may hold values from -6 to 6
- point_scale: float32 [8192], P('cols'), may hold values from 0.3 to 3
- env_owner: int32 [16384, 1], P('rows'), may hold values from 0 to 63; in each aligned block of 128 rows (0 to 127, 128 to 255, ...) at most 3 rows name the same one
- env_structure: int32 [16384], P('rows'), may hold values from 0 to 63
- row_weight: float32 [4096], P('rows'), may hold values from 0.01 to 0.1
- ridge_factor: float32 [1], replicated, may hold values from 0.05 to 0.5
Outputs:
- r_rows: float32 [128, 8192], P(None, 'cols')
- reduced: float32 [4096, 8192], P('rows', 'cols')
The draws below stay inside these ranges and needn't reach their ends.
Inputs may be any that keep to these rules, and one draw needn't show every extreme that they name: `env_owner`: in each aligned block of 128 environments, no owner is named by more than 3 of them.
All inputs are finite; a program needn't handle non-finite values.
Results may differ from the reference program's by a relative error of at most 0.0045.
Values may be sent and summed in bfloat16 or wider, within the bound.
No kernel may reach another device: no remote copies, remote signals or barrier semaphores. Data moves between devices by JAX's collectives and lax.ppermute only.
A program may use at most 64 MiB of HBM per device.

```python
import math
import jax
import jax.numpy as jnp
import numpy as np
from jax import lax

DESC = 1024
M = 8192
PW = 64
PANELS = 2
ENV_DEV = 256
EQ_DEV = 64
HALF = 128
CAP = 3
ENV = 16384
NEQ = 4096
N_ROWS = 64


def plant(result, key, least, top_value):
    place = [jax.random.randint(jax.random.fold_in(key, axis), (), 0, length) for axis, length in enumerate(result.shape)]
    widest = result.shape.index(max(result.shape))
    beside = place[:widest] + [(place[widest] + 1) % result.shape[widest]] + place[widest + 1:]
    return result.at[tuple(place)].set(least).at[tuple(beside)].set(top_value)


def level_of(own_key, dims, cuts, low, largest):
    def one(axis_at, parts):
        steps = jax.random.uniform(jax.random.fold_in(jax.random.fold_in(own_key, 6), axis_at), (parts,), jnp.float32, low / len(cuts), largest / len(cuts))
        return jnp.repeat(jnp.exp(steps), dims[axis_at] // parts).reshape((-1,) + (1,) * (len(dims) - axis_at - 1))

    level = one(*cuts[0])
    for cut in cuts[1:]:
        level = level * one(*cut)
    return level


def deal_out(key, own, number, rows, number_of, top, bound, skew):
    ranking = jax.random.permutation(key, number_of)
    crowded, common = shares(number_of, rows * top, bound, skew, True), shares(number_of, rows * top, bound, skew, False)
    places = jnp.arange(number_of)

    def named(lengths, turn):
        used = int((lengths > 0).sum())
        fixed = max(1, used // 4)
        passed = fixed + (places - fixed + turn * (used - fixed)) % max(1, number_of - fixed)
        return jnp.zeros((number_of,), jnp.int32).at[ranking[jnp.where(places < fixed, places, passed)]].set(jnp.asarray(lengths, jnp.int32))

    lengths = jnp.where(number % 4 == 0, named(crowded, number // 4), named(common, number - number // 4 - 1))
    mixed = jax.random.permutation(jax.random.fold_in(own, 3), number_of)
    source_of, sink = mixed[0:number_of // 2 * 2:2], mixed[1:number_of // 2 * 2:2]
    room = jnp.minimum(lengths[source_of] - 1, bound - lengths[sink]) // 2
    room = jnp.where((source_of == ranking[0]) | (sink == ranking[0]) | (lengths[sink] == 0), 0, jnp.maximum(room, 0))
    passed = jax.random.randint(jax.random.fold_in(own, 4), (number_of // 2,), 0, 1 << 20) % (room + 1)
    lengths = lengths.at[source_of].add(-passed).at[sink].add(passed)
    items = jnp.searchsorted(jnp.cumsum(lengths), jnp.arange(rows * top), side="right").astype(jnp.int32)
    grid = items.reshape(top, rows).T
    grid = grid[jax.random.permutation(jax.random.fold_in(own, 1), rows)]
    turn = jax.random.randint(jax.random.fold_in(own, 2), (rows, 1), 0, top)
    return jnp.take_along_axis(grid, (jnp.arange(top)[None, :] + turn) % top, axis=1)


def shares(amount, total, bound, skew, full):
    weights = [(1 << 20) // math.isqrt(rank ** skew) + 1 for rank in range(1, amount + 1)]
    largest = bound if full else min(bound, max(-(-total // amount), total * weights[0] // sum(weights)))
    least = 1 if total - largest >= amount - 1 else 0
    counts, rest = [largest] + [least] * (amount - 1), total - largest - least * (amount - 1)
    while rest > 0:
        free = [i for i in range(1, amount) if counts[i] < largest] or [i for i in range(1, amount) if counts[i] < bound]
        pool, left = sum([weights[i] for i in free]), rest
        for i in free:
            extra = min(bound - counts[i], max(1, left * weights[i] // pool), rest)
            counts[i] = counts[i] + extra
            rest = rest - extra
    return np.array(counts)


def scatter_about(stream_key, shape, scale, reach, shards=(), kind=jnp.bfloat16):
    array = jax.random.normal(stream_key, shape, jnp.float32) * scale
    if len(shards) > 0:
        array = level_of(stream_key, shape, shards, -0.22, 0.18) * array
    return jnp.clip(array, min=-reach, max=reach).astype(kind)


def setup_inputs(seed: int = 0) -> dict:
    key_list = jax.random.split(jax.random.key(seed), 8)
    descriptors = scatter_about(key_list[0], (ENV, DESC), 1.0, 6.0, ((0, 512),))
    sparse_points = scatter_about(key_list[1], (M, DESC), 1.0, 6.0, ((0, 8),))
    point_scale = jnp.clip(jnp.exp(math.log(3.0) - 2.3025851 * jax.random.uniform(key_list[2], (M,), jnp.float32) ** level_of(key_list[2], (M,), ((0, 8),), -0.2, 0.2)), 0.3, 3.0)
    env_owner_keys = jax.random.split(jax.random.fold_in(key_list[3], 1), ENV // HALF)
    env_owner_turns = jax.random.permutation(jax.random.fold_in(key_list[3], 3), ENV // HALF)
    env_owner = jax.vmap(lambda own, number: deal_out(jax.random.fold_in(key_list[3], 2), own, number, HALF, N_ROWS, 1, CAP, 2))(env_owner_keys, env_owner_turns).reshape((ENV, 1))
    env_structure = plant(jax.random.randint(key_list[4], (ENV,), 0, EQ_DEV), jax.random.fold_in(key_list[4], 1), 0, EQ_DEV - 1).astype(jnp.int32)
    row_weight = jnp.clip(jnp.exp(math.log(0.1) - 2.3025851 * jax.random.uniform(key_list[5], (NEQ,), jnp.float32) ** level_of(key_list[5], (NEQ,), ((0, 64),), -0.2, 0.2)), 0.01, 0.1)
    ridge_factor = jnp.clip(jnp.exp(jax.random.uniform(key_list[6], (1,), jnp.float32, math.log(0.05), math.log(0.5))), 0.05, 0.5)
    return {"descriptors": descriptors, "sparse_points": sparse_points, "point_scale": point_scale, "env_owner": env_owner, "env_structure": env_structure, "row_weight": row_weight, "ridge_factor": ridge_factor}


def inner_cols(left, right):
    return lax.dot_general(left.astype(jnp.float32), right.astype(jnp.float32), (((0,), (0,)), ((), ())), precision=lax.Precision.HIGHEST, preferred_element_type=jnp.float32)

def factor(gram_mat, ridge_factor):
    shift = ridge_factor[0] * jnp.trace(gram_mat) / PW + 1e-06
    chol_lower = jnp.linalg.cholesky(gram_mat + shift * jnp.eye(PW, dtype=jnp.float32))
    inverse = jax.scipy.linalg.solve_triangular(chol_lower, jnp.eye(PW, dtype=jnp.float32), lower=True)
    return (chol_lower, inverse)

def reference(descriptors, sparse_points, point_scale, env_owner, env_structure, row_weight, ridge_factor):
    dot_scale = DESC ** (-0.5)
    points = sparse_points.astype(jnp.float32)
    global_ids = (env_owner[:, 0].astype(jnp.int32) * EQ_DEV + env_structure.astype(jnp.int32)).astype(jnp.int32)
    desc_blocks = descriptors.reshape(N_ROWS, ENV_DEV, DESC)
    id_blocks = global_ids.reshape(N_ROWS, ENV_DEV)

    def add_block(sums, pieces):
        env_rows, env_ids = pieces
        products = jnp.dot(env_rows.astype(jnp.float32), points.T.astype(jnp.float32), precision=lax.Precision.HIGHEST, preferred_element_type=jnp.float32) * dot_scale
        squared = products * products
        kernel = (point_scale[None, :] * squared * squared).astype(jnp.bfloat16)
        kernel = lax.optimization_barrier(kernel).astype(jnp.float32)
        return (sums + jax.ops.segment_sum(kernel, env_ids, num_segments=NEQ), None)
    sums, _ = lax.scan(add_block, jnp.zeros((NEQ, M), jnp.float32), (desc_blocks, id_blocks))
    matrix = sums * row_weight[:, None]
    col_ids = jnp.arange(M, dtype=jnp.int32)[None, :]
    norm_scale = 1.0 / NEQ ** 0.5
    r_blocks = []
    for panel_idx in range(PANELS):
        first_col = panel_idx * PW
        panel_cols = matrix[:, first_col:first_col + PW]
        chol_lower, inverse = factor(inner_cols(panel_cols, panel_cols), ridge_factor)
        q_cols = jnp.dot(panel_cols.astype(jnp.float32), inverse.T.astype(jnp.float32), precision=lax.Precision.HIGHEST, preferred_element_type=jnp.float32)
        coupled = inner_cols(q_cols, matrix)
        later_mask = col_ids >= first_col + PW
        inside = (col_ids >= first_col) & (col_ids < first_col + PW)
        coupled = jnp.where(later_mask, coupled, 0.0)
        update = jnp.dot(q_cols.astype(jnp.float32), coupled.astype(jnp.float32), precision=lax.Precision.HIGHEST, preferred_element_type=jnp.float32)
        q_wide = jnp.pad(q_cols, ((0, 0), (first_col, M - first_col - PW)))
        matrix = jnp.where(inside, q_wide, matrix - update)
        r_wide = jnp.pad(chol_lower.T, ((0, 0), (first_col, M - first_col - PW)))
        r_blocks.append(jnp.where(inside, r_wide, coupled) * norm_scale)
    return (jnp.concatenate(r_blocks, axis=0), matrix)
```

```python
import functools
import math

import jax
import jax.numpy as jnp
from jax import lax
from jax.experimental import pallas as pl
from jax.experimental.pallas import tpu as pltpu
from jax.sharding import PartitionSpec as P

PW = 64
PANELS = 2
WIDE = PW * PANELS
CAP = 3
HALF = 128
LANES = 128
GROUP = 8
SLOTS = 2 * CAP
Y, Z = 4, 16
F32, BF16 = jnp.float32, jnp.bfloat16
HIGHEST = lax.Precision.HIGHEST
VMEM_LIMIT = 48 * 2**20


def dot(a, b, dims=((1,), (0,)), precision=None):
    return lax.dot_general(
        a, b, (dims, ((), ())), precision=precision, preferred_element_type=F32
    )


def iota(shape, dim):
    return lax.broadcasted_iota(jnp.int32, shape, dim)


def one_hot(condition):
    return condition.astype(F32).astype(BF16)


def called(kernel, out_shape, *args):
    return pl.pallas_call(
        kernel,
        out_shape=out_shape,
        compiler_params=pltpu.CompilerParams(vmem_limit_bytes=VMEM_LIMIT),
    )(*args)


def to_each(array, axis, groups=None):
    count = lax.axis_size(axis) if groups is None else len(groups[0])
    copies = jnp.broadcast_to(array, (count, *array.shape))
    return lax.all_to_all(
        copies, axis, split_axis=0, concat_axis=0, tiled=True, axis_index_groups=groups
    )


def pack_kernel(env_ref, owner_ref, structure_ref, out_ref, owners):
    owner = owner_ref[...]
    envs = owner.shape[1]
    matches = iota((owners, envs), 0) == owner
    earlier = (iota((envs, envs), 0) < iota((envs, envs), 1)) & (
        iota((envs, envs), 0) // HALF == iota((envs, envs), 1) // HALF
    )
    before = dot(one_hot(matches), one_hot(earlier))
    within = jnp.sum(jnp.where(matches, before, 0.0), axis=0, keepdims=True).astype(jnp.int32)
    place = (iota((1, envs), 1) // HALF) * CAP + within
    slot = owner * GROUP + place
    chosen = one_hot(iota((owners * GROUP, envs), 0) == slot)
    data = dot(chosen, env_ref[...].reshape(envs, LANES))
    named = jnp.where(matches, structure_ref[...], 0).astype(F32).astype(BF16)
    at = one_hot(iota((LANES, envs), 0) == place)
    labels = dot(named, at, ((1,), (1,)))
    spread = one_hot(iota((owners * GROUP, owners), 0) == iota((owners * GROUP, owners), 1) * GROUP + SLOTS)
    out_ref[...] = (data + dot(spread, labels.astype(BF16))).astype(BF16)


def unpack_kernel(got_ref, out_ref, label_ref):
    rows = got_ref.shape[0]
    sources = rows // GROUP
    slots = sources * SLOTS
    got = got_ref[...]
    slot, row = iota((slots, rows), 0), iota((slots, rows), 1)
    source, place = slot // SLOTS, slot % SLOTS
    out_ref[...] = dot(one_hot(row == source * GROUP + place), got).astype(BF16)
    named = dot(one_hot(row == source * GROUP + SLOTS), got)
    own = iota((slots, LANES), 1) == iota((slots, LANES), 0) % SLOTS
    label_ref[...] = jnp.sum(jnp.where(own, named, 0.0), axis=1, keepdims=True)


def equations_kernel(
    got_ref, label_ref, points_ref, scale_ref, extra_ref, weight_ref, matrix_ref, sums_ref, env_ref
):
    chunks, rows, _ = got_ref.shape
    slots = rows - WIDE
    eqs = weight_ref.shape[0]
    cols = points_ref.shape[0]
    for chunk in range(chunks):
        env_ref[:, chunk * LANES : (chunk + 1) * LANES] = got_ref[chunk]
    dot_scale = env_ref.shape[1] ** (-0.5)
    chosen = one_hot(label_ref[...].astype(jnp.int32) == iota((slots, eqs), 1))
    weight = weight_ref[...]

    def block(points, scale):
        z = dot(env_ref[0:slots, :], points, ((1,), (1,))) * dot_scale
        squared = z * z
        kernel = (scale * squared * squared).astype(BF16)
        return dot(chosen, kernel, ((0,), (0,))) * weight

    extra = extra_ref[...].astype(F32)
    panel = block(env_ref[slots:rows, :], extra[0:1] + extra[1:2] + extra[2:3])
    matrix_ref[:, cols : cols + WIDE] = panel
    gram = dot(panel, panel, ((0,), (0,)), HIGHEST)
    high = gram.astype(BF16)
    low = (gram - high.astype(F32)).astype(BF16)
    count = sums_ref.shape[0]
    row, col = iota((count * 8, 4 * count), 0), iota((count * 8, 4 * count), 1)
    spread = one_hot((row // 8 == col % count) & (row % 8 == col // count))
    gram_rows = dot(spread, jnp.concatenate([high, low], axis=0))
    sums_ref[:, 16:24, :] = gram_rows.astype(BF16).reshape(count, 8, LANES)
    step = 256
    for first in range(0, cols, step):
        part = block(points_ref[first : first + step, :], scale_ref[:, first : first + step])
        matrix_ref[:, first : first + step] = part
        cross = dot(panel, part, ((0,), (0,)), HIGHEST).astype(BF16)
        for at in range(0, step, LANES):
            k = (first + at) // LANES
            sums_ref[8 * k : 8 * k + 8, 0:16, :] = cross[:, at : at + LANES].reshape(8, 16, LANES)


def added_kernel(got_ref, out_ref):
    total = jnp.sum(got_ref[...].astype(F32), axis=0)
    out_ref[0:16, :] = total[0:16]
    out_ref[16:18, :] = total[16:18] + total[18:20]
    out_ref[18:24, :] = jnp.zeros((6, LANES), F32)


def eliminated(gram, shift):
    own = iota((PW, PW), 0) == iota((PW, PW), 1)
    eye = own.astype(F32)
    work = jnp.concatenate([gram + shift * eye, eye], axis=1)
    rows = iota((PW, 1), 0)
    for k in range(PW - 1):
        pivot_row = work[k : k + 1, :]
        ratio = work[:, k : k + 1] / work[k : k + 1, k : k + 1]
        work = work - jnp.where(rows > k, ratio, 0.0) * pivot_row
    pivots = jnp.sum(jnp.where(own, work[:, :PW], 0.0), axis=1, keepdims=True)
    work = work * lax.rsqrt(pivots)
    upper = jnp.where(iota((PW, PW), 0) <= iota((PW, PW), 1), work[:, :PW], 0.0)
    return upper, work[:, PW:]


def factor_kernel(total_ref, matrix_ref, ridge_ref, first_ref, r_ref, reduced_ref, norm_scale):
    ridge = ridge_ref[0]
    first = first_ref[0] == 0
    eqs, cols = reduced_ref.shape
    gram = jnp.concatenate([total_ref[:, 16, :], total_ref[:, 17, :]], axis=0)
    own = iota((PW, PW), 0) == iota((PW, PW), 1)

    def shift_of(a):
        return ridge * jnp.sum(jnp.where(own, a, 0.0)) / PW + 1e-06

    g00, g01, g11 = gram[:PW, :PW], gram[:PW, PW:], gram[PW:, PW:]
    shift0 = shift_of(g00)
    upper0, inverse0 = eliminated(g00, shift0)
    c01 = dot(inverse0, g01, precision=HIGHEST)
    w01 = dot(inverse0, c01, ((0,), (0,)), HIGHEST)
    gram1 = (
        g11
        - dot(c01, c01, ((0,), (0,)), HIGHEST)
        - shift0 * dot(w01, w01, ((0,), (0,)), HIGHEST)
    )
    upper1, inverse1 = eliminated(gram1, shift_of(gram1))
    panel = matrix_ref[:, cols : cols + WIDE]
    q0 = dot(panel[:, :PW], inverse0, ((1,), (1,)), HIGHEST)
    q1 = dot(panel[:, PW:] - dot(q0, c01, precision=HIGHEST), inverse1, ((1,), (1,)), HIGHEST)
    zero = jnp.zeros((PW, PW), F32)
    for k in range(cols // LANES):
        at = slice(k * LANES, (k + 1) * LANES)
        cross = total_ref[8 * k : 8 * k + 8, 0:16, :].reshape(WIDE, LANES)
        c0 = dot(inverse0, cross[:PW], precision=HIGHEST)
        w0 = dot(inverse0, c0, ((0,), (0,)), HIGHEST)
        rest = (
            cross[PW:]
            - dot(c01, c0, ((0,), (0,)), HIGHEST)
            - shift0 * dot(w01, w0, ((0,), (0,)), HIGHEST)
        )
        c1 = dot(inverse1, rest, precision=HIGHEST)
        left = matrix_ref[:, at] - dot(q0, c0, precision=HIGHEST) - dot(q1, c1, precision=HIGHEST)
        if k == 0:
            c0 = jnp.where(first, jnp.concatenate([upper0, c01], axis=1), c0)
            c1 = jnp.where(first, jnp.concatenate([zero, upper1], axis=1), c1)
            left = jnp.where(first, jnp.concatenate([q0, q1], axis=1), left)
        r_ref[0:PW, at] = c0 * norm_scale
        r_ref[PW:WIDE, at] = c1 * norm_scale
        reduced_ref[:, at] = left


def body(
    descriptors, sparse_points, point_scale, env_owner, env_structure, row_weight, ridge_factor
):
    owners, peers = lax.axis_size("rows"), lax.axis_size("cols")
    eqs, cols = row_weight.shape[0], point_scale.shape[0]
    mine = descriptors.shape[0]
    envs = mine * peers
    z_groups = [[y * Z + z for z in range(Z)] for y in range(Y)]
    y_groups = [[y * Z + z for y in range(Y)] for z in range(Z)]

    scale = point_scale[:WIDE]
    high = lax.reduce_precision(scale, 8, 7)
    middle = lax.reduce_precision(scale - high, 8, 7)
    low = scale - high - middle
    parts = jnp.zeros((16, WIDE), F32).at[0].set(high).at[1].set(middle).at[2].set(low)
    sent = jnp.concatenate([descriptors, sparse_points[:WIDE]], axis=0)
    sent = sent.reshape(mine + WIDE, peers, LANES).transpose(1, 0, 2)
    sent = jnp.concatenate(
        [sent, jnp.broadcast_to(parts.astype(BF16), (peers, 16, WIDE))], axis=1
    )
    got = lax.all_to_all(sent, "cols", split_axis=0, concat_axis=0, tiled=True)
    panel_part = got[0, mine : mine + WIDE]
    extra = got[0, mine + WIDE :]

    packed = called(
        functools.partial(pack_kernel, owners=owners),
        jax.ShapeDtypeStruct((owners * GROUP, LANES), BF16),
        got[:, :mine],
        env_owner.reshape(1, envs),
        env_structure.reshape(1, envs),
    )
    arrived = lax.all_to_all(packed, "rows", split_axis=0, concat_axis=0, tiled=True)
    slots = owners * SLOTS
    slot_rows, labels = called(
        unpack_kernel,
        (
            jax.ShapeDtypeStruct((slots, LANES), BF16),
            jax.ShapeDtypeStruct((slots, 1), F32),
        ),
        arrived,
    )
    gathered = to_each(jnp.concatenate([slot_rows, panel_part], axis=0), "cols")

    matrix, sums = pl.pallas_call(
        equations_kernel,
        out_shape=(
            jax.ShapeDtypeStruct((eqs, cols + WIDE), F32),
            jax.ShapeDtypeStruct((owners, 24, LANES), BF16),
        ),
        scratch_shapes=[pltpu.VMEM((slots + WIDE, peers * LANES), BF16)],
        compiler_params=pltpu.CompilerParams(vmem_limit_bytes=VMEM_LIMIT),
    )(
        gathered,
        labels,
        sparse_points,
        point_scale.reshape(1, cols),
        extra,
        row_weight.reshape(eqs, 1),
    )
    partial = lax.all_to_all(sums, "rows", split_axis=0, concat_axis=0, tiled=True)
    added = called(added_kernel, jax.ShapeDtypeStruct((24, LANES), F32), partial)
    total = to_each(to_each(added, "rows", z_groups), "rows", y_groups)
    total = total.reshape(owners, 24, LANES)

    vmem, smem = pl.BlockSpec(memory_space=pltpu.VMEM), pl.BlockSpec(memory_space=pltpu.SMEM)
    return pl.pallas_call(
        functools.partial(factor_kernel, norm_scale=1.0 / math.sqrt(owners * eqs)),
        out_shape=(
            jax.ShapeDtypeStruct((WIDE, cols), F32),
            jax.ShapeDtypeStruct((eqs, cols), F32),
        ),
        in_specs=[vmem, vmem, smem, smem],
        out_specs=(vmem, vmem),
        compiler_params=pltpu.CompilerParams(vmem_limit_bytes=VMEM_LIMIT),
    )(total, matrix, ridge_factor, lax.axis_index("cols").reshape(1))


def solution(mesh):
    return jax.shard_map(
        body,
        mesh=mesh,
        in_specs=(
            P(("rows", "cols"), None),
            P("cols", None),
            P("cols"),
            P("rows", None),
            P("rows"),
            P("rows"),
            P(),
        ),
        out_specs=(P(None, "cols"), P("rows", "cols")),
        check_vma=False,
    )
```

```python
import functools
import math

import jax
import jax.numpy as jnp
from jax import lax
from jax.experimental import pallas as pl
from jax.experimental.pallas import tpu as pltpu
from jax.sharding import PartitionSpec as P

PW = 64
PANELS = 2
WIDE = PW * PANELS
CAP = 3
HALF = 128
LANES = 128
GROUP = 8
SLOTS = 2 * CAP
STEP = 4
Y, Z = 4, 16
F32, BF16 = jnp.float32, jnp.bfloat16
HIGHEST = lax.Precision.HIGHEST
VMEM_LIMIT = 48 * 2**20


def dot(a, b, dims=((1,), (0,)), precision=None):
    return lax.dot_general(
        a, b, (dims, ((), ())), precision=precision, preferred_element_type=F32
    )


def iota(shape, dim):
    return lax.broadcasted_iota(jnp.int32, shape, dim)


def one_hot(condition):
    return condition.astype(F32).astype(BF16)


def called(kernel, out_shape, *args):
    return pl.pallas_call(
        kernel,
        out_shape=out_shape,
        compiler_params=pltpu.CompilerParams(vmem_limit_bytes=VMEM_LIMIT),
    )(*args)


def to_each(array, axis, groups=None):
    count = lax.axis_size(axis) if groups is None else len(groups[0])
    copies = jnp.broadcast_to(array, (count, *array.shape))
    return lax.all_to_all(
        copies, axis, split_axis=0, concat_axis=0, tiled=True, axis_index_groups=groups
    )


def pack_kernel(env_ref, owner_ref, structure_ref, out_ref, owners):
    owner = owner_ref[...]
    envs = owner.shape[1]
    matches = iota((owners, envs), 0) == owner
    earlier = (iota((envs, envs), 0) < iota((envs, envs), 1)) & (
        iota((envs, envs), 0) // HALF == iota((envs, envs), 1) // HALF
    )
    before = dot(one_hot(matches), one_hot(earlier))
    within = jnp.sum(jnp.where(matches, before, 0.0), axis=0, keepdims=True).astype(jnp.int32)
    place = (iota((1, envs), 1) // HALF) * CAP + within
    slot = owner * GROUP + place
    chosen = one_hot(iota((owners * GROUP, envs), 0) == slot)
    data = dot(chosen, env_ref[...].reshape(envs, LANES))
    named = jnp.where(matches, structure_ref[...], 0).astype(F32).astype(BF16)
    at = one_hot(iota((LANES, envs), 0) == place)
    labels = dot(named, at, ((1,), (1,)))
    spread = one_hot(iota((owners * GROUP, owners), 0) == iota((owners * GROUP, owners), 1) * GROUP + SLOTS)
    out_ref[...] = (data + dot(spread, labels.astype(BF16))).astype(BF16)


def unpack_kernel(got_ref, out_ref, label_ref):
    rows = got_ref.shape[0]
    sources = rows // GROUP
    slots = sources * SLOTS
    got = got_ref[...]
    slot, row = iota((slots, rows), 0), iota((slots, rows), 1)
    source, place = slot // SLOTS, slot % SLOTS
    data = dot(one_hot(row == source * GROUP + place), got).astype(BF16)
    for copy in range(out_ref.shape[0]):
        out_ref[copy] = data
    named = dot(one_hot(row == source * GROUP + SLOTS), got)
    own = iota((slots, LANES), 1) == iota((slots, LANES), 0) % SLOTS
    label_ref[...] = jnp.sum(jnp.where(own, named, 0.0), axis=1, keepdims=True)


def equations_kernel(
    core_ref,
    own_ref,
    other_ref,
    label_ref,
    points_ref,
    scale_ref,
    panel_ref,
    weight_ref,
    matrix_ref,
    sums_ref,
    env_ref,
):
    chips, slots, _ = own_ref.shape
    eqs = weight_ref.shape[0]
    cols = points_ref.shape[0]
    core = core_ref[0]
    for chip in range(chips):
        at = pl.multiple_of((2 * chip + core) * LANES, LANES)
        env_ref[:, pl.ds(at, LANES)] = own_ref[chip]
        at = pl.multiple_of((2 * chip + 1 - core) * LANES, LANES)
        env_ref[:, pl.ds(at, LANES)] = other_ref[chip]
    dot_scale = env_ref.shape[1] ** (-0.5)
    chosen = one_hot(label_ref[...].astype(jnp.int32) == iota((slots, eqs), 1))
    weight = weight_ref[...]

    def block(points, scale):
        z = dot(env_ref[...], points, ((1,), (1,))) * dot_scale
        squared = z * z
        kernel = (scale * squared * squared).astype(BF16)
        return dot(chosen, kernel, ((0,), (0,))) * weight

    parts = panel_ref[WIDE:, 0:WIDE].astype(F32)
    panel = block(panel_ref[0:WIDE, :], parts[0:1] + parts[1:2] + parts[2:3])
    matrix_ref[:, cols : cols + WIDE] = panel
    gram = dot(panel, panel, ((0,), (0,)), HIGHEST)
    high = gram.astype(BF16)
    low = (gram - high.astype(F32)).astype(BF16)
    members, length, _ = sums_ref.shape
    own_rows = length - 2 * WIDE
    for member in range(members):
        sums_ref[member, own_rows : own_rows + WIDE] = high
        sums_ref[member, own_rows + WIDE : length] = low
    step = 256
    for first in range(0, cols, step):
        part = block(points_ref[first : first + step, :], scale_ref[:, first : first + step])
        matrix_ref[:, first : first + step] = part
        cross = dot(panel, part, ((0,), (0,)), HIGHEST).astype(BF16)
        for at in range(0, step, LANES):
            member, start = divmod((first + at) // LANES * WIDE, own_rows)
            sums_ref[member, start : start + WIDE] = cross[:, at : at + LANES]


def near_kernel(got_ref, out_ref):
    total = jnp.sum(got_ref[...].astype(F32), axis=0)
    count, length, _ = out_ref.shape
    own_rows = total.shape[0] - 2 * WIDE
    own = own_rows // count
    gram = total[own_rows : own_rows + WIDE] + total[own_rows + WIDE :]
    out_ref[:, 0:own] = total[:own_rows].reshape(count, own, LANES)
    out_ref[:, own:length] = gram.reshape(count, length - own, LANES)


def far_kernel(got_ref, out_ref):
    total = jnp.sum(got_ref[...], axis=0)
    for copy in range(out_ref.shape[0]):
        out_ref[copy] = total


def eliminated(gram, shift):
    own = iota((PW, PW), 0) == iota((PW, PW), 1)
    eye = own.astype(F32)
    work = jnp.concatenate([gram + shift * eye, eye], axis=1)
    rows = iota((PW, 1), 0)
    for k in range(0, PW, STEP):
        cols = [jnp.broadcast_to(work[:, k + j : k + j + 1], (PW, WIDE)) for j in range(STEP)]
        pivot = [work[k + i : k + i + 1, :] for i in range(STEP)]
        inner = [[cols[j][k + i : k + i + 1, :] for j in range(STEP)] for i in range(STEP)]
        for a in range(STEP):
            inverse = 1.0 / inner[a][a]
            for i in range(a + 1, STEP):
                ratio = inner[i][a] * inverse
                pivot[i] = pivot[i] - ratio * pivot[a]
                for j in range(a + 1, STEP):
                    inner[i][j] = inner[i][j] - ratio * inner[a][j]
            cols[a] = cols[a] * inverse
            for j in range(a + 1, STEP):
                cols[j] = cols[j] - cols[a] * inner[a][j]
        below = work
        for a in range(STEP):
            below = below - cols[a] * pivot[a]
        work = jnp.where(rows >= k + STEP, below, work)
        for a in range(STEP):
            work = jnp.where(rows == k + a, pivot[a], work)
    pivots = jnp.sum(jnp.where(own, work[:, :PW], 0.0), axis=1, keepdims=True)
    work = work * lax.rsqrt(pivots)
    upper = jnp.where(iota((PW, PW), 0) <= iota((PW, PW), 1), work[:, :PW], 0.0)
    return upper, work[:, PW:]


def factor_kernel(gram_ref, ridge_ref, terms_ref, turn_ref, upper_ref):
    ridge = ridge_ref[0]
    count, length, _ = gram_ref.shape
    gram = gram_ref[:, length - WIDE // count : length].reshape(WIDE, WIDE)
    own = iota((PW, PW), 0) == iota((PW, PW), 1)

    def shift_of(a):
        return ridge * jnp.sum(jnp.where(own, a, 0.0)) / PW + 1e-06

    g00, g01, g11 = gram[:PW, :PW], gram[:PW, PW:], gram[PW:, PW:]
    shift0 = shift_of(g00)
    upper0, inverse0 = eliminated(g00, shift0)
    c01 = dot(inverse0, g01, precision=HIGHEST)
    w01 = dot(inverse0, c01, ((0,), (0,)), HIGHEST)
    gram1 = (
        g11
        - dot(c01, c01, ((0,), (0,)), HIGHEST)
        - shift0 * dot(w01, w01, ((0,), (0,)), HIGHEST)
    )
    upper1, inverse1 = eliminated(gram1, shift_of(gram1))
    mixed = c01 + shift0 * dot(inverse0, w01, precision=HIGHEST)
    both = jnp.concatenate([mixed, c01], axis=1)
    taken = dot(both, inverse0, ((0,), (0,)), HIGHEST)
    zero = jnp.zeros((PW, PW), F32)
    terms_ref[0:PW, :] = jnp.concatenate([inverse0, zero], axis=1)
    terms_ref[PW:WIDE, :] = jnp.concatenate(
        [-dot(inverse1, taken[:PW], precision=HIGHEST), inverse1], axis=1
    )
    turn_ref[0:PW, :] = jnp.concatenate([inverse0, zero], axis=1)
    turn_ref[PW:WIDE, :] = jnp.concatenate(
        [-dot(inverse1, taken[PW:], precision=HIGHEST), inverse1], axis=1
    )
    upper_ref[0:PW, :] = jnp.concatenate([upper0, c01], axis=1)
    upper_ref[PW:WIDE, :] = jnp.concatenate([zero, upper1], axis=1)


def final_kernel(
    first_ref, total_ref, terms_ref, turn_ref, upper_ref, matrix_ref, r_ref, reduced_ref, norm_scale
):
    first = first_ref[0] == 0
    cols = reduced_ref.shape[1]
    terms = terms_ref[...]
    q = dot(matrix_ref[:, cols : cols + WIDE], turn_ref[...], ((1,), (1,)), HIGHEST)
    step = 256
    for k in range(cols // step):
        at = slice(k * step, (k + 1) * step)
        cross = jnp.concatenate(
            [
                total_ref[8 * j : 8 * j + 8].reshape(WIDE, LANES)
                for j in range(k * step // LANES, (k + 1) * step // LANES)
            ],
            axis=1,
        )
        coupled = dot(terms, cross, precision=HIGHEST)
        r_ref[:, at] = coupled * norm_scale
        reduced_ref[:, at] = matrix_ref[:, at] - dot(q, coupled, precision=HIGHEST)

    @pl.when(first)
    def _():
        r_ref[:, 0:WIDE] = upper_ref[...] * norm_scale
        reduced_ref[:, 0:WIDE] = q


def body(
    descriptors, sparse_points, point_scale, env_owner, env_structure, row_weight, ridge_factor
):
    owners, peers = lax.axis_size("rows"), lax.axis_size("cols")
    eqs, cols = row_weight.shape[0], point_scale.shape[0]
    mine = descriptors.shape[0]
    envs = mine * peers
    z_groups = [[y * Z + z for z in range(Z)] for y in range(Y)]
    y_groups = [[y * Z + z for y in range(Y)] for z in range(Z)]

    scale = point_scale[:WIDE]
    high = lax.reduce_precision(scale, 8, 7)
    middle = lax.reduce_precision(scale - high, 8, 7)
    low = scale - high - middle
    parts = jnp.pad(jnp.stack([high, middle, low]), ((0, 13), (0, peers * LANES - WIDE)))
    panel = jnp.concatenate([sparse_points[:WIDE], parts.astype(BF16)], axis=0)

    sent = descriptors.reshape(mine, peers, LANES).transpose(1, 0, 2)
    got = lax.all_to_all(sent, "cols", split_axis=0, concat_axis=0, tiled=True)

    packed = called(
        functools.partial(pack_kernel, owners=owners),
        jax.ShapeDtypeStruct((owners * GROUP, LANES), BF16),
        got,
        env_owner.reshape(1, envs),
        env_structure.reshape(1, envs),
    )
    col = lax.axis_index("cols")
    near = jnp.where(col == 0, panel, lax.ppermute(panel, "cols", [(0, 1)]))
    for chip in range(1, peers // 2):
        reached = lax.ppermute(near, "cols", [(0, 2 * chip), (1, 2 * chip + 1)])
        panel = near + reached if chip == 1 else panel + reached
    arrived = lax.all_to_all(packed, "rows", split_axis=0, concat_axis=0, tiled=True)
    arrived, panel = lax.optimization_barrier((arrived, panel))
    slots = owners * SLOTS
    slot_rows, labels = called(
        unpack_kernel,
        (
            jax.ShapeDtypeStruct((peers // 2, slots, LANES), BF16),
            jax.ShapeDtypeStruct((slots, 1), F32),
        ),
        arrived,
    )
    own = lax.all_to_all(
        slot_rows,
        "cols",
        split_axis=0,
        concat_axis=0,
        tiled=True,
        axis_index_groups=[list(range(0, peers, 2)), list(range(1, peers, 2))],
    )
    other = lax.ppermute(own, "cols", [(c, c ^ 1) for c in range(peers)])

    vmem, smem = pl.BlockSpec(memory_space=pltpu.VMEM), pl.BlockSpec(memory_space=pltpu.SMEM)
    params = pltpu.CompilerParams(vmem_limit_bytes=VMEM_LIMIT)
    own_rows = cols // LANES * WIDE // Y
    matrix, sums = pl.pallas_call(
        equations_kernel,
        out_shape=(
            jax.ShapeDtypeStruct((eqs, cols + WIDE), F32),
            jax.ShapeDtypeStruct((Y, own_rows + 2 * WIDE, LANES), BF16),
        ),
        in_specs=[smem] + [vmem] * 7,
        out_specs=(vmem, vmem),
        scratch_shapes=[pltpu.VMEM((slots, peers * LANES), BF16)],
        compiler_params=params,
    )(
        (col % 2).reshape(1),
        own,
        other,
        labels,
        sparse_points,
        point_scale.reshape(1, cols),
        panel,
        row_weight.reshape(eqs, 1),
    )
    def exchanged(array, groups):
        return lax.all_to_all(
            array, "rows", split_axis=0, concat_axis=0, tiled=True, axis_index_groups=groups
        )

    own = own_rows // Z
    length = own + WIDE // Z
    message = jax.ShapeDtypeStruct((Z, length, LANES), F32)
    summed = called(near_kernel, message, exchanged(sums, y_groups))
    summed = called(far_kernel, message, exchanged(summed, z_groups))
    column = exchanged(summed, z_groups)
    total = to_each(column[:, :own], "rows", y_groups)
    total = total.reshape(owners, own, LANES)

    square = jax.ShapeDtypeStruct((WIDE, WIDE), F32)
    terms, turn, upper = pl.pallas_call(
        factor_kernel,
        out_shape=(square, square, square),
        in_specs=[vmem, smem],
        out_specs=(vmem, vmem, vmem),
        compiler_params=params,
        cost_estimate=pl.CostEstimate(flops=8_000_000_000, bytes_accessed=262144, transcendentals=0),
    )(column, ridge_factor)
    return pl.pallas_call(
        functools.partial(final_kernel, norm_scale=1.0 / math.sqrt(owners * eqs)),
        out_shape=(
            jax.ShapeDtypeStruct((WIDE, cols), F32),
            jax.ShapeDtypeStruct((eqs, cols), F32),
        ),
        in_specs=[smem] + [vmem] * 5,
        out_specs=(vmem, vmem),
        compiler_params=params,
    )(col.reshape(1), total, terms, turn, upper, matrix)


def solution(mesh):
    return jax.shard_map(
        body,
        mesh=mesh,
        in_specs=(
            P(("rows", "cols"), None),
            P("cols", None),
            P("cols"),
            P("rows", None),
            P("rows"),
            P("rows"),
            P(),
        ),
        out_specs=(P(None, "cols"), P("rows", "cols")),
        check_vma=False,
    )
```

```python
import functools
import math

import jax
import jax.numpy as jnp
from jax import lax
from jax.experimental import pallas as pl
from jax.experimental.pallas import tpu as pltpu
from jax.sharding import PartitionSpec as P

PW = 64
PANELS = 2
WIDE = PW * PANELS
CAP = 3
HALF = 128
LANES = 128
GROUP = 8
SLOTS = 2 * CAP
STEP = 4
Y, Z = 4, 16
F32, BF16 = jnp.float32, jnp.bfloat16
HIGHEST = lax.Precision.HIGHEST
VMEM_LIMIT = 20 * 2**20


def dot(a, b, dims=((1,), (0,)), precision=None):
    return lax.dot_general(
        a, b, (dims, ((), ())), precision=precision, preferred_element_type=F32
    )


def iota(shape, dim):
    return lax.broadcasted_iota(jnp.int32, shape, dim)


def one_hot(condition):
    return condition.astype(F32).astype(BF16)


def called(kernel, out_shape, *args):
    return pl.pallas_call(
        kernel,
        out_shape=out_shape,
        compiler_params=pltpu.CompilerParams(vmem_limit_bytes=VMEM_LIMIT),
    )(*args)


def to_each(array, axis, groups=None):
    count = lax.axis_size(axis) if groups is None else len(groups[0])
    copies = jnp.broadcast_to(array, (count, *array.shape))
    return lax.all_to_all(
        copies, axis, split_axis=0, concat_axis=0, tiled=True, axis_index_groups=groups
    )


def pack_kernel(env_ref, owner_ref, structure_ref, out_ref, owners):
    owner = owner_ref[...]
    envs = owner.shape[1]
    matches = iota((owners, envs), 0) == owner
    earlier = (iota((envs, envs), 0) < iota((envs, envs), 1)) & (
        iota((envs, envs), 0) // HALF == iota((envs, envs), 1) // HALF
    )
    before = dot(one_hot(matches), one_hot(earlier))
    within = jnp.sum(jnp.where(matches, before, 0.0), axis=0, keepdims=True).astype(jnp.int32)
    place = (iota((1, envs), 1) // HALF) * CAP + within
    slot = owner * GROUP + place
    chosen = one_hot(iota((owners * GROUP, envs), 0) == slot)
    data = dot(chosen, env_ref[...].reshape(envs, LANES))
    named = jnp.where(matches, structure_ref[...], 0).astype(F32).astype(BF16)
    at = one_hot(iota((LANES, envs), 0) == place)
    labels = dot(named, at, ((1,), (1,)))
    spread = one_hot(iota((owners * GROUP, owners), 0) == iota((owners * GROUP, owners), 1) * GROUP + SLOTS)
    out_ref[...] = (data + dot(spread, labels.astype(BF16))).astype(BF16)


def unpack_kernel(got_ref, out_ref, label_ref):
    rows = got_ref.shape[0]
    sources = rows // GROUP
    slots = sources * SLOTS
    got = got_ref[...]
    slot, row = iota((slots, rows), 0), iota((slots, rows), 1)
    source, place = slot // SLOTS, slot % SLOTS
    data = dot(one_hot(row == source * GROUP + place), got).astype(BF16)
    for copy in range(out_ref.shape[0]):
        out_ref[copy] = data
    source, row = iota((sources, rows), 0), iota((sources, rows), 1)
    label_ref[...] = dot(one_hot(row == source * GROUP + SLOTS), got).astype(BF16)


def equations_kernel(
    core_ref,
    own_ref,
    other_ref,
    label_ref,
    points_ref,
    scale_ref,
    panel_ref,
    weight_ref,
    matrix_ref,
    sums_ref,
    env_ref,
):
    chips, slots, _ = own_ref.shape
    eqs = weight_ref.shape[1]
    cols = points_ref.shape[0]
    core = core_ref[0]
    for chip in range(chips):
        at = pl.multiple_of((2 * chip + core) * LANES, LANES)
        env_ref[:, pl.ds(at, LANES)] = own_ref[chip]
        at = pl.multiple_of((2 * chip + 1 - core) * LANES, LANES)
        env_ref[:, pl.ds(at, LANES)] = other_ref[chip]
    dot_scale = env_ref.shape[1] ** (-0.5)
    sources = label_ref.shape[0]
    source = one_hot(iota((slots, sources), 0) // SLOTS == iota((slots, sources), 1))
    named = dot(source, label_ref[...])
    mine = iota((slots, LANES), 1) == iota((slots, LANES), 0) % SLOTS
    label = jnp.sum(jnp.where(mine, named, 0.0), axis=1, keepdims=True)
    chosen = one_hot(label.astype(jnp.int32) == iota((slots, eqs), 1))
    diagonal = jnp.where(iota((eqs, eqs), 0) == iota((eqs, eqs), 1), weight_ref[...], 0.0)
    weight = jnp.sum(diagonal, axis=1, keepdims=True)

    def block(points, scale):
        z = dot(env_ref[...], points, ((1,), (1,))) * dot_scale
        squared = z * z
        kernel = (scale * squared * squared).astype(BF16)
        return dot(chosen, kernel, ((0,), (0,))) * weight

    parts = panel_ref[WIDE:, 0:WIDE].astype(F32)
    panel = block(panel_ref[0:WIDE, :], parts[0:1] + parts[1:2] + parts[2:3])
    matrix_ref[:, cols : cols + WIDE] = panel
    gram = dot(panel, panel, ((0,), (0,)), HIGHEST)
    high = gram.astype(BF16)
    low = (gram - high.astype(F32)).astype(BF16)
    members, length, _ = sums_ref.shape
    own_rows = length - 2 * WIDE
    for member in range(members):
        sums_ref[member, own_rows : own_rows + WIDE] = high
        sums_ref[member, own_rows + WIDE : length] = low
    step = 256
    for first in range(0, cols, step):
        part = block(points_ref[first : first + step, :], scale_ref[:, first : first + step])
        matrix_ref[:, first : first + step] = part
        cross = dot(panel, part, ((0,), (0,)), HIGHEST).astype(BF16)
        for at in range(0, step, LANES):
            member, start = divmod((first + at) // LANES * WIDE, own_rows)
            sums_ref[member, start : start + WIDE] = cross[:, at : at + LANES]


def near_kernel(got_ref, out_ref):
    total = jnp.sum(got_ref[...].astype(F32), axis=0)
    count, length, _ = out_ref.shape
    own_rows = total.shape[0] - 2 * WIDE
    own = own_rows // count
    gram = total[own_rows : own_rows + WIDE] + total[own_rows + WIDE :]
    out_ref[:, 0:own] = total[:own_rows].reshape(count, own, LANES)
    out_ref[:, own:length] = gram.reshape(count, length - own, LANES)


def far_kernel(got_ref, out_ref):
    total = jnp.sum(got_ref[...], axis=0)
    for copy in range(out_ref.shape[0]):
        out_ref[copy] = total


def eliminated(gram, shift):
    own = iota((PW, PW), 0) == iota((PW, PW), 1)
    eye = own.astype(F32)
    work = jnp.concatenate([gram + shift * eye, eye], axis=1)
    rows = iota((PW, 1), 0)
    for k in range(0, PW, STEP):
        cols = [jnp.broadcast_to(work[:, k + j : k + j + 1], (PW, WIDE)) for j in range(STEP)]
        pivot = [work[k + i : k + i + 1, :] for i in range(STEP)]
        inner = [[cols[j][k + i : k + i + 1, :] for j in range(STEP)] for i in range(STEP)]
        for a in range(STEP):
            inverse = 1.0 / inner[a][a]
            for i in range(a + 1, STEP):
                ratio = inner[i][a] * inverse
                pivot[i] = pivot[i] - ratio * pivot[a]
                for j in range(a + 1, STEP):
                    inner[i][j] = inner[i][j] - ratio * inner[a][j]
            cols[a] = cols[a] * inverse
            for j in range(a + 1, STEP):
                cols[j] = cols[j] - cols[a] * inner[a][j]
        below = work
        for a in range(STEP):
            below = below - cols[a] * pivot[a]
        work = jnp.where(rows >= k + STEP, below, work)
        for a in range(STEP):
            work = jnp.where(rows == k + a, pivot[a], work)
    pivots = jnp.sum(jnp.where(own, work[:, :PW], 0.0), axis=1, keepdims=True)
    work = work * lax.rsqrt(pivots)
    upper = jnp.where(iota((PW, PW), 0) <= iota((PW, PW), 1), work[:, :PW], 0.0)
    return upper, work[:, PW:]


def factor_kernel(gram_ref, ridge_ref, terms_ref, turn_ref, upper_ref):
    ridge = ridge_ref[0]
    count, length, _ = gram_ref.shape
    gram = gram_ref[:, length - WIDE // count : length].reshape(WIDE, WIDE)
    own = iota((PW, PW), 0) == iota((PW, PW), 1)

    def shift_of(a):
        return ridge * jnp.sum(jnp.where(own, a, 0.0)) / PW + 1e-06

    g00, g01, g11 = gram[:PW, :PW], gram[:PW, PW:], gram[PW:, PW:]
    shift0 = shift_of(g00)
    upper0, inverse0 = eliminated(g00, shift0)
    c01 = dot(inverse0, g01, precision=HIGHEST)
    w01 = dot(inverse0, c01, ((0,), (0,)), HIGHEST)
    gram1 = (
        g11
        - dot(c01, c01, ((0,), (0,)), HIGHEST)
        - shift0 * dot(w01, w01, ((0,), (0,)), HIGHEST)
    )
    upper1, inverse1 = eliminated(gram1, shift_of(gram1))
    mixed = c01 + shift0 * dot(inverse0, w01, precision=HIGHEST)
    both = jnp.concatenate([mixed, c01], axis=1)
    taken = dot(both, inverse0, ((0,), (0,)), HIGHEST)
    zero = jnp.zeros((PW, PW), F32)
    terms_ref[0:PW, :] = jnp.concatenate([inverse0, zero], axis=1)
    terms_ref[PW:WIDE, :] = jnp.concatenate(
        [-dot(inverse1, taken[:PW], precision=HIGHEST), inverse1], axis=1
    )
    turn_ref[0:PW, :] = jnp.concatenate([inverse0, zero], axis=1)
    turn_ref[PW:WIDE, :] = jnp.concatenate(
        [-dot(inverse1, taken[PW:], precision=HIGHEST), inverse1], axis=1
    )
    upper_ref[0:PW, :] = jnp.concatenate([upper0, c01], axis=1)
    upper_ref[PW:WIDE, :] = jnp.concatenate([zero, upper1], axis=1)


def final_kernel(
    first_ref, total_ref, terms_ref, turn_ref, upper_ref, matrix_ref, r_ref, reduced_ref, norm_scale
):
    first = first_ref[0] == 0
    cols = reduced_ref.shape[1]
    terms = terms_ref[...]
    q = dot(matrix_ref[:, cols : cols + WIDE], turn_ref[...], ((1,), (1,)), HIGHEST)
    step = 256
    for k in range(cols // step):
        at = slice(k * step, (k + 1) * step)
        cross = jnp.concatenate(
            [
                total_ref[8 * j : 8 * j + 8].reshape(WIDE, LANES)
                for j in range(k * step // LANES, (k + 1) * step // LANES)
            ],
            axis=1,
        )
        coupled = dot(terms, cross, precision=HIGHEST)
        r_ref[:, at] = coupled * norm_scale
        reduced_ref[:, at] = matrix_ref[:, at] - dot(q, coupled, precision=HIGHEST)

    @pl.when(first)
    def _():
        r_ref[:, 0:WIDE] = upper_ref[...] * norm_scale
        reduced_ref[:, 0:WIDE] = q


def body(
    descriptors, sparse_points, point_scale, env_owner, env_structure, row_weight, ridge_factor
):
    owners, peers = lax.axis_size("rows"), lax.axis_size("cols")
    eqs, cols = row_weight.shape[0], point_scale.shape[0]
    mine = descriptors.shape[0]
    envs = mine * peers
    z_groups = [[y * Z + z for z in range(Z)] for y in range(Y)]
    y_groups = [[y * Z + z for y in range(Y)] for z in range(Z)]

    scale = point_scale[:WIDE]
    high = lax.reduce_precision(scale, 8, 7)
    middle = lax.reduce_precision(scale - high, 8, 7)
    low = scale - high - middle
    parts = jnp.pad(jnp.stack([high, middle, low]), ((0, 13), (0, peers * LANES - WIDE)))
    panel = jnp.concatenate([sparse_points[:WIDE], parts.astype(BF16)], axis=0)

    sent = descriptors.reshape(mine, peers, LANES).transpose(1, 0, 2)
    got = lax.all_to_all(sent, "cols", split_axis=0, concat_axis=0, tiled=True)

    packed = called(
        functools.partial(pack_kernel, owners=owners),
        jax.ShapeDtypeStruct((owners * GROUP, LANES), BF16),
        got,
        env_owner.reshape(1, envs),
        env_structure.reshape(1, envs),
    )
    packed, panel = lax.optimization_barrier((packed, panel))
    col = lax.axis_index("cols")
    near = jnp.where(col == 0, panel, lax.ppermute(panel, "cols", [(0, 1)]))
    for chip in range(1, peers // 2):
        reached = lax.ppermute(near, "cols", [(0, 2 * chip), (1, 2 * chip + 1)])
        panel = near + reached if chip == 1 else panel + reached
    arrived = lax.all_to_all(packed, "rows", split_axis=0, concat_axis=0, tiled=True)
    slots = owners * SLOTS
    slot_rows, labels = called(
        unpack_kernel,
        (
            jax.ShapeDtypeStruct((peers // 2, slots, LANES), BF16),
            jax.ShapeDtypeStruct((owners, LANES), BF16),
        ),
        arrived,
    )
    slot_rows, panel = lax.optimization_barrier((slot_rows, panel))
    own = lax.all_to_all(
        slot_rows,
        "cols",
        split_axis=0,
        concat_axis=0,
        tiled=True,
        axis_index_groups=[list(range(0, peers, 2)), list(range(1, peers, 2))],
    )
    other = lax.ppermute(own, "cols", [(c, c ^ 1) for c in range(peers)])

    vmem, smem = pl.BlockSpec(memory_space=pltpu.VMEM), pl.BlockSpec(memory_space=pltpu.SMEM)
    params = pltpu.CompilerParams(vmem_limit_bytes=VMEM_LIMIT)
    own_rows = cols // LANES * WIDE // Y
    matrix, sums = pl.pallas_call(
        equations_kernel,
        out_shape=(
            jax.ShapeDtypeStruct((eqs, cols + WIDE), F32),
            jax.ShapeDtypeStruct((Y, own_rows + 2 * WIDE, LANES), BF16),
        ),
        in_specs=[smem] + [vmem] * 7,
        out_specs=(vmem, vmem),
        scratch_shapes=[pltpu.VMEM((slots, peers * LANES), BF16)],
        compiler_params=params,
    )(
        (col % 2).reshape(1),
        own,
        other,
        labels,
        sparse_points,
        point_scale.reshape(1, cols),
        panel,
        row_weight.reshape(1, eqs),
    )
    def exchanged(array, groups):
        return lax.all_to_all(
            array, "rows", split_axis=0, concat_axis=0, tiled=True, axis_index_groups=groups
        )

    own = own_rows // Z
    length = own + WIDE // Z
    message = jax.ShapeDtypeStruct((Z, length, LANES), F32)
    summed = called(near_kernel, message, exchanged(sums, y_groups))
    summed = called(far_kernel, message, exchanged(summed, z_groups))
    column = exchanged(summed, z_groups)
    total = to_each(column[:, :own], "rows", y_groups)
    total = total.reshape(owners, own, LANES)

    square = jax.ShapeDtypeStruct((WIDE, WIDE), F32)
    terms, turn, upper = pl.pallas_call(
        factor_kernel,
        out_shape=(square, square, square),
        in_specs=[vmem, smem],
        out_specs=(vmem, vmem, vmem),
        compiler_params=params,
        cost_estimate=pl.CostEstimate(flops=8_000_000_000, bytes_accessed=262144, transcendentals=0),
    )(column, ridge_factor)
    return pl.pallas_call(
        functools.partial(final_kernel, norm_scale=1.0 / math.sqrt(owners * eqs)),
        out_shape=(
            jax.ShapeDtypeStruct((WIDE, cols), F32),
            jax.ShapeDtypeStruct((eqs, cols), F32),
        ),
        in_specs=[smem] + [vmem] * 5,
        out_specs=(vmem, vmem),
        compiler_params=params,
    )(col.reshape(1), total, terms, turn, upper, matrix)


def solution(mesh):
    return jax.shard_map(
        body,
        mesh=mesh,
        in_specs=(
            P(("rows", "cols"), None),
            P("cols", None),
            P("cols"),
            P("rows", None),
            P("rows"),
            P("rows"),
            P(),
        ),
        out_specs=(P(None, "cols"), P("rows", "cols")),
        check_vma=False,
    )
```

```python
import functools
import math

import jax
import jax.numpy as jnp
from jax import lax
from jax.experimental import pallas as pl
from jax.experimental.pallas import tpu as pltpu
from jax.sharding import PartitionSpec as P

PW = 64
PANELS = 2
WIDE = PW * PANELS
CAP = 3
HALF = 128
LANES = 128
GROUP = 8
SLOTS = 2 * CAP
STEP = 4
Y, Z = 4, 16
F32, BF16 = jnp.float32, jnp.bfloat16
HIGHEST = lax.Precision.HIGHEST
VMEM_LIMIT = 20 * 2**20


def dot(a, b, dims=((1,), (0,)), precision=None):
    return lax.dot_general(
        a, b, (dims, ((), ())), precision=precision, preferred_element_type=F32
    )


def iota(shape, dim):
    return lax.broadcasted_iota(jnp.int32, shape, dim)


def one_hot(condition):
    return condition.astype(F32).astype(BF16)


def called(kernel, out_shape, *args):
    return pl.pallas_call(
        kernel,
        out_shape=out_shape,
        compiler_params=pltpu.CompilerParams(vmem_limit_bytes=VMEM_LIMIT),
    )(*args)


def to_each(array, axis, groups=None):
    count = lax.axis_size(axis) if groups is None else len(groups[0])
    copies = jnp.broadcast_to(array, (count, *array.shape))
    return lax.all_to_all(
        copies, axis, split_axis=0, concat_axis=0, tiled=True, axis_index_groups=groups
    )


def pack_kernel(env_ref, equation_ref, out_ref, owners, eqs):
    owner, structure = equation_ref[...] // eqs, equation_ref[...] % eqs
    envs = owner.shape[1]
    matches = iota((owners, envs), 0) == owner
    earlier = (iota((envs, envs), 0) < iota((envs, envs), 1)) & (
        iota((envs, envs), 0) // HALF == iota((envs, envs), 1) // HALF
    )
    before = dot(one_hot(matches), one_hot(earlier))
    within = jnp.sum(jnp.where(matches, before, 0.0), axis=0, keepdims=True).astype(jnp.int32)
    place = (iota((1, envs), 1) // HALF) * CAP + within
    slot = owner * GROUP + place
    chosen = one_hot(iota((owners * GROUP, envs), 0) == slot)
    data = dot(chosen, env_ref[...].reshape(envs, LANES))
    named = jnp.where(matches, structure, 0).astype(F32).astype(BF16)
    at = one_hot(iota((LANES, envs), 0) == place)
    labels = dot(named, at, ((1,), (1,)))
    spread = one_hot(iota((owners * GROUP, owners), 0) == iota((owners * GROUP, owners), 1) * GROUP + SLOTS)
    out_ref[...] = (data + dot(spread, labels.astype(BF16))).astype(BF16)


def unpack_kernel(got_ref, out_ref, label_ref):
    rows = got_ref.shape[0]
    sources = rows // GROUP
    slots = sources * SLOTS
    got = got_ref[...]
    slot, row = iota((slots, rows), 0), iota((slots, rows), 1)
    source, place = slot // SLOTS, slot % SLOTS
    data = dot(one_hot(row == source * GROUP + place), got).astype(BF16)
    for copy in range(out_ref.shape[0]):
        out_ref[copy] = data
    source, row = iota((sources, rows), 0), iota((sources, rows), 1)
    label_ref[...] = dot(one_hot(row == source * GROUP + SLOTS), got).astype(BF16)


def equations_kernel(
    core_ref,
    own_ref,
    other_ref,
    label_ref,
    points_ref,
    scale_ref,
    panel_ref,
    matrix_ref,
    sums_ref,
    env_ref,
):
    chips, slots, _ = own_ref.shape
    cols = points_ref.shape[0]
    eqs = scale_ref.shape[1] - cols
    core = core_ref[0]
    for chip in range(chips):
        at = pl.multiple_of((2 * chip + core) * LANES, LANES)
        env_ref[:, pl.ds(at, LANES)] = own_ref[chip]
        at = pl.multiple_of((2 * chip + 1 - core) * LANES, LANES)
        env_ref[:, pl.ds(at, LANES)] = other_ref[chip]
    dot_scale = env_ref.shape[1] ** (-0.5)
    sources = label_ref.shape[0]
    source = one_hot(iota((slots, sources), 0) // SLOTS == iota((slots, sources), 1))
    named = dot(source, label_ref[...])
    mine = iota((slots, LANES), 1) == iota((slots, LANES), 0) % SLOTS
    label = jnp.sum(jnp.where(mine, named, 0.0), axis=1, keepdims=True)
    chosen = one_hot(label.astype(jnp.int32) == iota((slots, eqs), 1))
    diagonal = jnp.where(iota((eqs, eqs), 0) == iota((eqs, eqs), 1), scale_ref[:, cols:], 0.0)
    weight = jnp.sum(diagonal, axis=1, keepdims=True)

    def block(points, scale):
        z = dot(env_ref[...], points, ((1,), (1,))) * dot_scale
        squared = z * z
        kernel = (scale * squared * squared).astype(BF16)
        return dot(chosen, kernel, ((0,), (0,))) * weight

    parts = panel_ref[WIDE:, 0:WIDE].astype(F32)
    panel = block(panel_ref[0:WIDE, :], parts[0:1] + parts[1:2] + parts[2:3])
    matrix_ref[:, cols : cols + WIDE] = panel
    gram = dot(panel, panel, ((0,), (0,)), HIGHEST)
    high = gram.astype(BF16)
    low = (gram - high.astype(F32)).astype(BF16)
    members, length, _ = sums_ref.shape
    own_rows = length - 2 * WIDE
    for member in range(members):
        sums_ref[member, own_rows : own_rows + WIDE] = high
        sums_ref[member, own_rows + WIDE : length] = low
    step = 256
    for first in range(0, cols, step):
        part = block(points_ref[first : first + step, :], scale_ref[:, first : first + step])
        matrix_ref[:, first : first + step] = part
        cross = dot(panel, part, ((0,), (0,)), HIGHEST).astype(BF16)
        for at in range(0, step, LANES):
            member, start = divmod((first + at) // LANES * WIDE, own_rows)
            sums_ref[member, start : start + WIDE] = cross[:, at : at + LANES]


def near_kernel(got_ref, out_ref):
    total = jnp.sum(got_ref[...].astype(F32), axis=0)
    count, length, _ = out_ref.shape
    own_rows = total.shape[0] - 2 * WIDE
    own = own_rows // count
    gram = total[own_rows : own_rows + WIDE] + total[own_rows + WIDE :]
    out_ref[:, 0:own] = total[:own_rows].reshape(count, own, LANES)
    out_ref[:, own:length] = gram.reshape(count, length - own, LANES)


def far_kernel(got_ref, out_ref):
    total = jnp.sum(got_ref[...], axis=0)
    for copy in range(out_ref.shape[0]):
        out_ref[copy] = total


def eliminated(gram, shift):
    own = iota((PW, PW), 0) == iota((PW, PW), 1)
    eye = own.astype(F32)
    work = jnp.concatenate([gram + shift * eye, eye], axis=1)
    rows = iota((PW, 1), 0)
    for k in range(0, PW, STEP):
        cols = [jnp.broadcast_to(work[:, k + j : k + j + 1], (PW, WIDE)) for j in range(STEP)]
        pivot = [work[k + i : k + i + 1, :] for i in range(STEP)]
        inner = [[cols[j][k + i : k + i + 1, :] for j in range(STEP)] for i in range(STEP)]
        for a in range(STEP):
            inverse = 1.0 / inner[a][a]
            for i in range(a + 1, STEP):
                ratio = inner[i][a] * inverse
                pivot[i] = pivot[i] - ratio * pivot[a]
                for j in range(a + 1, STEP):
                    inner[i][j] = inner[i][j] - ratio * inner[a][j]
            cols[a] = cols[a] * inverse
            for j in range(a + 1, STEP):
                cols[j] = cols[j] - cols[a] * inner[a][j]
        below = work
        for a in range(STEP):
            below = below - cols[a] * pivot[a]
        work = jnp.where(rows >= k + STEP, below, work)
        for a in range(STEP):
            work = jnp.where(rows == k + a, pivot[a], work)
    pivots = jnp.sum(jnp.where(own, work[:, :PW], 0.0), axis=1, keepdims=True)
    work = work * lax.rsqrt(pivots)
    upper = jnp.where(iota((PW, PW), 0) <= iota((PW, PW), 1), work[:, :PW], 0.0)
    return upper, work[:, PW:]


def factor_kernel(gram_ref, ridge_ref, terms_ref, turn_ref, upper_ref):
    ridge = ridge_ref[0]
    count, length, _ = gram_ref.shape
    gram = gram_ref[:, length - WIDE // count : length].reshape(WIDE, WIDE)
    own = iota((PW, PW), 0) == iota((PW, PW), 1)

    def shift_of(a):
        return ridge * jnp.sum(jnp.where(own, a, 0.0)) / PW + 1e-06

    g00, g01, g11 = gram[:PW, :PW], gram[:PW, PW:], gram[PW:, PW:]
    shift0 = shift_of(g00)
    upper0, inverse0 = eliminated(g00, shift0)
    c01 = dot(inverse0, g01, precision=HIGHEST)
    w01 = dot(inverse0, c01, ((0,), (0,)), HIGHEST)
    gram1 = (
        g11
        - dot(c01, c01, ((0,), (0,)), HIGHEST)
        - shift0 * dot(w01, w01, ((0,), (0,)), HIGHEST)
    )
    upper1, inverse1 = eliminated(gram1, shift_of(gram1))
    mixed = c01 + shift0 * dot(inverse0, w01, precision=HIGHEST)
    both = jnp.concatenate([mixed, c01], axis=1)
    taken = dot(both, inverse0, ((0,), (0,)), HIGHEST)
    zero = jnp.zeros((PW, PW), F32)
    terms_ref[0:PW, :] = jnp.concatenate([inverse0, zero], axis=1)
    terms_ref[PW:WIDE, :] = jnp.concatenate(
        [-dot(inverse1, taken[:PW], precision=HIGHEST), inverse1], axis=1
    )
    turn_ref[0:PW, :] = jnp.concatenate([inverse0, zero], axis=1)
    turn_ref[PW:WIDE, :] = jnp.concatenate(
        [-dot(inverse1, taken[PW:], precision=HIGHEST), inverse1], axis=1
    )
    upper_ref[0:PW, :] = jnp.concatenate([upper0, c01], axis=1)
    upper_ref[PW:WIDE, :] = jnp.concatenate([zero, upper1], axis=1)


def final_kernel(
    first_ref, total_ref, terms_ref, turn_ref, upper_ref, matrix_ref, r_ref, reduced_ref, norm_scale
):
    first = first_ref[0] == 0
    cols = reduced_ref.shape[1]
    terms = terms_ref[...]
    q = dot(matrix_ref[:, cols : cols + WIDE], turn_ref[...], ((1,), (1,)), HIGHEST)
    step = 256
    for k in range(cols // step):
        at = slice(k * step, (k + 1) * step)
        cross = jnp.concatenate(
            [
                total_ref[8 * j : 8 * j + 8].reshape(WIDE, LANES)
                for j in range(k * step // LANES, (k + 1) * step // LANES)
            ],
            axis=1,
        )
        coupled = dot(terms, cross, precision=HIGHEST)
        r_ref[:, at] = coupled * norm_scale
        reduced_ref[:, at] = matrix_ref[:, at] - dot(q, coupled, precision=HIGHEST)

    @pl.when(first)
    def _():
        r_ref[:, 0:WIDE] = upper_ref[...] * norm_scale
        reduced_ref[:, 0:WIDE] = q


def body(
    descriptors, sparse_points, point_scale, env_owner, env_structure, row_weight, ridge_factor
):
    owners, peers = lax.axis_size("rows"), lax.axis_size("cols")
    eqs, cols = row_weight.shape[0], point_scale.shape[0]
    mine = descriptors.shape[0]
    envs = mine * peers
    z_groups = [[y * Z + z for z in range(Z)] for y in range(Y)]
    y_groups = [[y * Z + z for y in range(Y)] for z in range(Z)]

    scale = point_scale[:WIDE]
    high = lax.reduce_precision(scale, 8, 7)
    middle = lax.reduce_precision(scale - high, 8, 7)
    low = scale - high - middle
    parts = jnp.pad(jnp.stack([high, middle, low]), ((0, 13), (0, peers * LANES - WIDE)))
    panel = jnp.concatenate([sparse_points[:WIDE], parts.astype(BF16)], axis=0)

    sent = descriptors.reshape(mine, peers, LANES).transpose(1, 0, 2)
    got = lax.all_to_all(sent, "cols", split_axis=0, concat_axis=0, tiled=True)

    packed = called(
        functools.partial(pack_kernel, owners=owners, eqs=eqs),
        jax.ShapeDtypeStruct((owners * GROUP, LANES), BF16),
        got,
        (env_owner[:, 0] * eqs + env_structure).reshape(1, envs),
    )
    col = lax.axis_index("cols")
    near = jnp.where(col == 0, panel, lax.ppermute(panel, "cols", [(0, 1)]))
    for chip in range(1, peers // 2):
        reached = lax.ppermute(near, "cols", [(0, 2 * chip), (1, 2 * chip + 1)])
        panel = near + reached if chip == 1 else panel + reached
    arrived = lax.all_to_all(packed, "rows", split_axis=0, concat_axis=0, tiled=True)
    slots = owners * SLOTS
    slot_rows, labels = called(
        unpack_kernel,
        (
            jax.ShapeDtypeStruct((peers // 2, slots, LANES), BF16),
            jax.ShapeDtypeStruct((owners, LANES), BF16),
        ),
        arrived,
    )
    own = lax.all_to_all(
        slot_rows,
        "cols",
        split_axis=0,
        concat_axis=0,
        tiled=True,
        axis_index_groups=[list(range(0, peers, 2)), list(range(1, peers, 2))],
    )
    other = lax.ppermute(own, "cols", [(c, c ^ 1) for c in range(peers)])

    vmem, smem = pl.BlockSpec(memory_space=pltpu.VMEM), pl.BlockSpec(memory_space=pltpu.SMEM)
    params = pltpu.CompilerParams(vmem_limit_bytes=VMEM_LIMIT)
    own_rows = cols // LANES * WIDE // Y
    matrix, sums = pl.pallas_call(
        equations_kernel,
        out_shape=(
            jax.ShapeDtypeStruct((eqs, cols + WIDE), F32),
            jax.ShapeDtypeStruct((Y, own_rows + 2 * WIDE, LANES), BF16),
        ),
        in_specs=[smem] + [vmem] * 6,
        out_specs=(vmem, vmem),
        scratch_shapes=[pltpu.VMEM((slots, peers * LANES), BF16)],
        compiler_params=params,
    )(
        (col % 2).reshape(1),
        own,
        other,
        labels,
        sparse_points,
        jnp.concatenate([point_scale, row_weight]).reshape(1, cols + eqs),
        panel,
    )
    def exchanged(array, groups):
        return lax.all_to_all(
            array, "rows", split_axis=0, concat_axis=0, tiled=True, axis_index_groups=groups
        )

    own = own_rows // Z
    length = own + WIDE // Z
    message = jax.ShapeDtypeStruct((Z, length, LANES), F32)
    summed = called(near_kernel, message, exchanged(sums, y_groups))
    summed = called(far_kernel, message, exchanged(summed, z_groups))
    column = exchanged(summed, z_groups)
    total = to_each(column[:, :own], "rows", y_groups)
    total = total.reshape(owners, own, LANES)

    square = jax.ShapeDtypeStruct((WIDE, WIDE), F32)
    terms, turn, upper = pl.pallas_call(
        factor_kernel,
        out_shape=(square, square, square),
        in_specs=[vmem, smem],
        out_specs=(vmem, vmem, vmem),
        compiler_params=params,
        cost_estimate=pl.CostEstimate(flops=8_000_000_000, bytes_accessed=262144, transcendentals=0),
    )(column, ridge_factor)
    return pl.pallas_call(
        functools.partial(final_kernel, norm_scale=1.0 / math.sqrt(owners * eqs)),
        out_shape=(
            jax.ShapeDtypeStruct((WIDE, cols), F32),
            jax.ShapeDtypeStruct((eqs, cols), F32),
        ),
        in_specs=[smem] + [vmem] * 5,
        out_specs=(vmem, vmem),
        compiler_params=params,
    )(col.reshape(1), total, terms, turn, upper, matrix)


def solution(mesh):
    return jax.shard_map(
        body,
        mesh=mesh,
        in_specs=(
            P(("rows", "cols"), None),
            P("cols", None),
            P("cols"),
            P("rows", None),
            P("rows"),
            P("rows"),
            P(),
        ),
        out_specs=(P(None, "cols"), P("rows", "cols")),
        check_vma=False,
    )
```

```python
import functools
import math

import jax
import jax.numpy as jnp
from jax import lax
from jax.experimental import pallas as pl
from jax.experimental.pallas import tpu as pltpu
from jax.sharding import PartitionSpec as P

PW = 64
PANELS = 2
WIDE = PW * PANELS
CAP = 3
HALF = 128
LANES = 128
GROUP = 8
SLOTS = 2 * CAP
STEP = 4
Y, Z = 4, 16
F32, BF16 = jnp.float32, jnp.bfloat16
HIGHEST = lax.Precision.HIGHEST
VMEM_LIMIT = 20 * 2**20


def dot(a, b, dims=((1,), (0,)), precision=None):
    return lax.dot_general(
        a, b, (dims, ((), ())), precision=precision, preferred_element_type=F32
    )


def iota(shape, dim):
    return lax.broadcasted_iota(jnp.int32, shape, dim)


def one_hot(condition):
    return condition.astype(F32).astype(BF16)


def called(kernel, out_shape, *args):
    return pl.pallas_call(
        kernel,
        out_shape=out_shape,
        compiler_params=pltpu.CompilerParams(vmem_limit_bytes=VMEM_LIMIT),
    )(*args)


def to_each(array, axis, groups=None):
    count = lax.axis_size(axis) if groups is None else len(groups[0])
    copies = jnp.broadcast_to(array, (count, *array.shape))
    return lax.all_to_all(
        copies, axis, split_axis=0, concat_axis=0, tiled=True, axis_index_groups=groups
    )


def first_kernel(env_ref, points_ref, scale_ref, out_ref):
    mine, wide = env_ref.shape[0], points_ref.shape[0]
    scale = scale_ref[...]
    high = scale.astype(BF16).astype(F32)
    middle = (scale - high).astype(BF16).astype(F32)
    low = scale - high - middle
    row = iota((16, wide), 0)
    parts = jnp.where(row == 0, high, jnp.where(row == 1, middle, jnp.where(row == 2, low, 0.0)))
    for peer in range(out_ref.shape[0]):
        at = slice(peer * LANES, (peer + 1) * LANES)
        out_ref[peer, 0:mine] = env_ref[:, at]
        out_ref[peer, mine : mine + wide] = points_ref[:, at]
        out_ref[peer, mine + wide :] = parts.astype(BF16)


def pack_kernel(env_ref, equation_ref, out_ref, owners, eqs):
    owner, structure = equation_ref[...] // eqs, equation_ref[...] % eqs
    envs = owner.shape[1]
    matches = iota((owners, envs), 0) == owner
    earlier = (iota((envs, envs), 0) < iota((envs, envs), 1)) & (
        iota((envs, envs), 0) // HALF == iota((envs, envs), 1) // HALF
    )
    before = dot(one_hot(matches), one_hot(earlier))
    within = jnp.sum(jnp.where(matches, before, 0.0), axis=0, keepdims=True).astype(jnp.int32)
    place = (iota((1, envs), 1) // HALF) * CAP + within
    slot = owner * GROUP + place
    chosen = one_hot(iota((owners * GROUP, envs), 0) == slot)
    data = dot(chosen, env_ref[:, 0 : envs // env_ref.shape[0]].reshape(envs, LANES))
    named = jnp.where(matches, structure, 0).astype(F32).astype(BF16)
    at = one_hot(iota((LANES, envs), 0) == place)
    labels = dot(named, at, ((1,), (1,)))
    spread = one_hot(iota((owners * GROUP, owners), 0) == iota((owners * GROUP, owners), 1) * GROUP + SLOTS)
    out_ref[...] = (data + dot(spread, labels.astype(BF16))).astype(BF16)


def unpack_kernel(got_ref, panel_ref, out_ref, label_ref):
    rows = got_ref.shape[0]
    sources = rows // GROUP
    slots = sources * SLOTS
    got = got_ref[...]
    slot, row = iota((slots, rows), 0), iota((slots, rows), 1)
    source, place = slot // SLOTS, slot % SLOTS
    data = dot(one_hot(row == source * GROUP + place), got).astype(BF16)
    for copy in range(out_ref.shape[0]):
        out_ref[copy, 0:slots] = data
        out_ref[copy, slots:] = panel_ref[...]
    source, row = iota((sources, rows), 0), iota((sources, rows), 1)
    label_ref[...] = dot(one_hot(row == source * GROUP + SLOTS), got).astype(BF16)


def equations_kernel(
    core_ref,
    own_ref,
    other_ref,
    label_ref,
    points_ref,
    scale_ref,
    panel_ref,
    matrix_ref,
    sums_ref,
    env_ref,
):
    chips, rows, _ = own_ref.shape
    slots = rows - WIDE
    cols = points_ref.shape[0]
    eqs = scale_ref.shape[1] - cols
    core = core_ref[0]
    for chip in range(chips):
        at = pl.multiple_of((2 * chip + core) * LANES, LANES)
        env_ref[:, pl.ds(at, LANES)] = own_ref[chip]
        at = pl.multiple_of((2 * chip + 1 - core) * LANES, LANES)
        env_ref[:, pl.ds(at, LANES)] = other_ref[chip]
    dot_scale = env_ref.shape[1] ** (-0.5)
    sources = label_ref.shape[0]
    source = one_hot(iota((slots, sources), 0) // SLOTS == iota((slots, sources), 1))
    named = dot(source, label_ref[...])
    mine = iota((slots, LANES), 1) == iota((slots, LANES), 0) % SLOTS
    label = jnp.sum(jnp.where(mine, named, 0.0), axis=1, keepdims=True)
    chosen = one_hot(label.astype(jnp.int32) == iota((slots, eqs), 1))
    diagonal = jnp.where(iota((eqs, eqs), 0) == iota((eqs, eqs), 1), scale_ref[:, cols:], 0.0)
    weight = jnp.sum(diagonal, axis=1, keepdims=True)

    def block(points, scale):
        z = dot(env_ref[0:slots, :], points, ((1,), (1,))) * dot_scale
        squared = z * z
        kernel = (scale * squared * squared).astype(BF16)
        return dot(chosen, kernel, ((0,), (0,))) * weight

    parts = panel_ref[...].astype(F32)
    panel = block(env_ref[slots:rows, :], parts[0:1] + parts[1:2] + parts[2:3])
    matrix_ref[:, cols : cols + WIDE] = panel
    gram = dot(panel, panel, ((0,), (0,)), HIGHEST)
    high = gram.astype(BF16)
    low = (gram - high.astype(F32)).astype(BF16)
    members, length, _ = sums_ref.shape
    own_rows = length - 2 * WIDE
    for member in range(members):
        sums_ref[member, own_rows : own_rows + WIDE] = high
        sums_ref[member, own_rows + WIDE : length] = low
    step = 256
    for first in range(0, cols, step):
        part = block(points_ref[first : first + step, :], scale_ref[:, first : first + step])
        matrix_ref[:, first : first + step] = part
        cross = dot(panel, part, ((0,), (0,)), HIGHEST).astype(BF16)
        for at in range(0, step, LANES):
            member, start = divmod((first + at) // LANES * WIDE, own_rows)
            sums_ref[member, start : start + WIDE] = cross[:, at : at + LANES]


def near_kernel(got_ref, out_ref):
    total = jnp.sum(got_ref[...].astype(F32), axis=0)
    count, length, _ = out_ref.shape
    own_rows = total.shape[0] - 2 * WIDE
    own = own_rows // count
    gram = total[own_rows : own_rows + WIDE] + total[own_rows + WIDE :]
    out_ref[:, 0:own] = total[:own_rows].reshape(count, own, LANES)
    out_ref[:, own:length] = gram.reshape(count, length - own, LANES)


def far_kernel(got_ref, out_ref):
    total = jnp.sum(got_ref[...], axis=0)
    for copy in range(out_ref.shape[0]):
        out_ref[copy] = total


def eliminated(gram, shift):
    own = iota((PW, PW), 0) == iota((PW, PW), 1)
    eye = own.astype(F32)
    work = jnp.concatenate([gram + shift * eye, eye], axis=1)
    rows = iota((PW, 1), 0)
    for k in range(0, PW, STEP):
        cols = [jnp.broadcast_to(work[:, k + j : k + j + 1], (PW, WIDE)) for j in range(STEP)]
        pivot = [work[k + i : k + i + 1, :] for i in range(STEP)]
        inner = [[cols[j][k + i : k + i + 1, :] for j in range(STEP)] for i in range(STEP)]
        for a in range(STEP):
            inverse = 1.0 / inner[a][a]
            for i in range(a + 1, STEP):
                ratio = inner[i][a] * inverse
                pivot[i] = pivot[i] - ratio * pivot[a]
                for j in range(a + 1, STEP):
                    inner[i][j] = inner[i][j] - ratio * inner[a][j]
            cols[a] = cols[a] * inverse
            for j in range(a + 1, STEP):
                cols[j] = cols[j] - cols[a] * inner[a][j]
        below = work
        for a in range(STEP):
            below = below - cols[a] * pivot[a]
        work = jnp.where(rows >= k + STEP, below, work)
        for a in range(STEP):
            work = jnp.where(rows == k + a, pivot[a], work)
    pivots = jnp.sum(jnp.where(own, work[:, :PW], 0.0), axis=1, keepdims=True)
    work = work * lax.rsqrt(pivots)
    upper = jnp.where(iota((PW, PW), 0) <= iota((PW, PW), 1), work[:, :PW], 0.0)
    return upper, work[:, PW:]


def factor_kernel(gram_ref, ridge_ref, terms_ref, turn_ref, upper_ref):
    ridge = ridge_ref[0]
    count, length, _ = gram_ref.shape
    gram = gram_ref[:, length - WIDE // count : length].reshape(WIDE, WIDE)
    own = iota((PW, PW), 0) == iota((PW, PW), 1)

    def shift_of(a):
        return ridge * jnp.sum(jnp.where(own, a, 0.0)) / PW + 1e-06

    g00, g01, g11 = gram[:PW, :PW], gram[:PW, PW:], gram[PW:, PW:]
    shift0 = shift_of(g00)
    upper0, inverse0 = eliminated(g00, shift0)
    c01 = dot(inverse0, g01, precision=HIGHEST)
    w01 = dot(inverse0, c01, ((0,), (0,)), HIGHEST)
    gram1 = (
        g11
        - dot(c01, c01, ((0,), (0,)), HIGHEST)
        - shift0 * dot(w01, w01, ((0,), (0,)), HIGHEST)
    )
    upper1, inverse1 = eliminated(gram1, shift_of(gram1))
    mixed = c01 + shift0 * dot(inverse0, w01, precision=HIGHEST)
    both = jnp.concatenate([mixed, c01], axis=1)
    taken = dot(both, inverse0, ((0,), (0,)), HIGHEST)
    zero = jnp.zeros((PW, PW), F32)
    terms_ref[0:PW, :] = jnp.concatenate([inverse0, zero], axis=1)
    terms_ref[PW:WIDE, :] = jnp.concatenate(
        [-dot(inverse1, taken[:PW], precision=HIGHEST), inverse1], axis=1
    )
    turn_ref[0:PW, :] = jnp.concatenate([inverse0, zero], axis=1)
    turn_ref[PW:WIDE, :] = jnp.concatenate(
        [-dot(inverse1, taken[PW:], precision=HIGHEST), inverse1], axis=1
    )
    upper_ref[0:PW, :] = jnp.concatenate([upper0, c01], axis=1)
    upper_ref[PW:WIDE, :] = jnp.concatenate([zero, upper1], axis=1)


def final_kernel(
    first_ref, total_ref, terms_ref, turn_ref, upper_ref, matrix_ref, r_ref, reduced_ref, norm_scale
):
    first = first_ref[0] == 0
    cols = reduced_ref.shape[1]
    terms = terms_ref[...]
    q = dot(matrix_ref[:, cols : cols + WIDE], turn_ref[...], ((1,), (1,)), HIGHEST)
    step = 256
    for k in range(cols // step):
        at = slice(k * step, (k + 1) * step)
        cross = jnp.concatenate(
            [
                total_ref[8 * j : 8 * j + 8].reshape(WIDE, LANES)
                for j in range(k * step // LANES, (k + 1) * step // LANES)
            ],
            axis=1,
        )
        coupled = dot(terms, cross, precision=HIGHEST)
        r_ref[:, at] = coupled * norm_scale
        reduced_ref[:, at] = matrix_ref[:, at] - dot(q, coupled, precision=HIGHEST)

    @pl.when(first)
    def _():
        r_ref[:, 0:WIDE] = upper_ref[...] * norm_scale
        reduced_ref[:, 0:WIDE] = q


def body(
    descriptors, sparse_points, point_scale, env_owner, env_structure, row_weight, ridge_factor
):
    owners, peers = lax.axis_size("rows"), lax.axis_size("cols")
    eqs, cols = row_weight.shape[0], point_scale.shape[0]
    mine = descriptors.shape[0]
    envs = mine * peers
    z_groups = [[y * Z + z for z in range(Z)] for y in range(Y)]
    y_groups = [[y * Z + z for y in range(Y)] for z in range(Z)]

    length = mine + WIDE + 16
    sent = pl.pallas_call(
        first_kernel,
        out_shape=jax.ShapeDtypeStruct((peers, length, LANES), BF16),
        grid=(1,),
        in_specs=[
            pl.BlockSpec((mine, peers * LANES), lambda i: (0, 0)),
            pl.BlockSpec((WIDE, peers * LANES), lambda i: (0, 0)),
            pl.BlockSpec((1, WIDE), lambda i: (0, 0)),
        ],
        out_specs=pl.BlockSpec((peers, length, LANES), lambda i: (0, 0, 0)),
        compiler_params=pltpu.CompilerParams(vmem_limit_bytes=60 * 2**20),
    )(descriptors, sparse_points, point_scale.reshape(1, cols))
    got = lax.all_to_all(sent, "cols", split_axis=0, concat_axis=0, tiled=True)
    panel_part, parts = got[0, mine : mine + WIDE], got[0, mine + WIDE :]

    packed = called(
        functools.partial(pack_kernel, owners=owners, eqs=eqs),
        jax.ShapeDtypeStruct((owners * GROUP, LANES), BF16),
        got,
        (env_owner[:, 0] * eqs + env_structure).reshape(1, envs),
    )
    col = lax.axis_index("cols")
    arrived = lax.all_to_all(packed, "rows", split_axis=0, concat_axis=0, tiled=True)
    slots = owners * SLOTS
    slot_rows, labels = called(
        unpack_kernel,
        (
            jax.ShapeDtypeStruct((peers // 2, slots + WIDE, LANES), BF16),
            jax.ShapeDtypeStruct((owners, LANES), BF16),
        ),
        arrived,
        panel_part,
    )
    own = lax.all_to_all(
        slot_rows,
        "cols",
        split_axis=0,
        concat_axis=0,
        tiled=True,
        axis_index_groups=[list(range(0, peers, 2)), list(range(1, peers, 2))],
    )
    other = lax.ppermute(own, "cols", [(c, c ^ 1) for c in range(peers)])

    vmem, smem = pl.BlockSpec(memory_space=pltpu.VMEM), pl.BlockSpec(memory_space=pltpu.SMEM)
    params = pltpu.CompilerParams(vmem_limit_bytes=VMEM_LIMIT)
    own_rows = cols // LANES * WIDE // Y
    matrix, sums = pl.pallas_call(
        equations_kernel,
        out_shape=(
            jax.ShapeDtypeStruct((eqs, cols + WIDE), F32),
            jax.ShapeDtypeStruct((Y, own_rows + 2 * WIDE, LANES), BF16),
        ),
        in_specs=[smem] + [vmem] * 6,
        out_specs=(vmem, vmem),
        scratch_shapes=[pltpu.VMEM((slots + WIDE, peers * LANES), BF16)],
        compiler_params=params,
    )(
        (col % 2).reshape(1),
        own,
        other,
        labels,
        sparse_points,
        jnp.concatenate([point_scale, row_weight]).reshape(1, cols + eqs),
        parts,
    )
    def exchanged(array, groups):
        return lax.all_to_all(
            array, "rows", split_axis=0, concat_axis=0, tiled=True, axis_index_groups=groups
        )

    own = own_rows // Z
    length = own + WIDE // Z
    message = jax.ShapeDtypeStruct((Z, length, LANES), F32)
    summed = called(near_kernel, message, exchanged(sums, y_groups))
    summed = called(far_kernel, message, exchanged(summed, z_groups))
    column = exchanged(summed, z_groups)
    total = to_each(column[:, :own], "rows", y_groups)
    total = total.reshape(owners, own, LANES)

    square = jax.ShapeDtypeStruct((WIDE, WIDE), F32)
    terms, turn, upper = pl.pallas_call(
        factor_kernel,
        out_shape=(square, square, square),
        in_specs=[vmem, smem],
        out_specs=(vmem, vmem, vmem),
        compiler_params=params,
        cost_estimate=pl.CostEstimate(flops=8_000_000_000, bytes_accessed=262144, transcendentals=0),
    )(column, ridge_factor)
    return pl.pallas_call(
        functools.partial(final_kernel, norm_scale=1.0 / math.sqrt(owners * eqs)),
        out_shape=(
            jax.ShapeDtypeStruct((WIDE, cols), F32),
            jax.ShapeDtypeStruct((eqs, cols), F32),
        ),
        in_specs=[smem] + [vmem] * 5,
        out_specs=(vmem, vmem),
        compiler_params=params,
    )(col.reshape(1), total, terms, turn, upper, matrix)


def solution(mesh):
    return jax.shard_map(
        body,
        mesh=mesh,
        in_specs=(
            P(("rows", "cols"), None),
            P("cols", None),
            P("cols"),
            P("rows", None),
            P("rows"),
            P("rows"),
            P(),
        ),
        out_specs=(P(None, "cols"), P("rows", "cols")),
        check_vma=False,
    )
```

```python
import functools
import math

import jax
import jax.numpy as jnp
from jax import lax
from jax.experimental import pallas as pl
from jax.experimental.pallas import tpu as pltpu
from jax.sharding import PartitionSpec as P

PW = 64
PANELS = 2
WIDE = PW * PANELS
CAP = 3
HALF = 128
LANES = 128
GROUP = 8
SLOTS = 2 * CAP
STEP = 4
Y, Z = 4, 16
F32, BF16, F16 = jnp.float32, jnp.bfloat16, jnp.float16
TOP = 14
HIGHEST = lax.Precision.HIGHEST
VMEM_LIMIT = 20 * 2**20


def dot(a, b, dims=((1,), (0,)), precision=None):
    return lax.dot_general(
        a, b, (dims, ((), ())), precision=precision, preferred_element_type=F32
    )


def iota(shape, dim):
    return lax.broadcasted_iota(jnp.int32, shape, dim)


def one_hot(condition):
    return condition.astype(F32).astype(BF16)


def called(kernel, out_shape, *args):
    return pl.pallas_call(
        kernel,
        out_shape=out_shape,
        compiler_params=pltpu.CompilerParams(vmem_limit_bytes=VMEM_LIMIT),
    )(*args)


def to_each(array, axis, groups=None):
    count = lax.axis_size(axis) if groups is None else len(groups[0])
    copies = jnp.broadcast_to(array, (count, *array.shape))
    return lax.all_to_all(
        copies, axis, split_axis=0, concat_axis=0, tiled=True, axis_index_groups=groups
    )


def first_kernel(env_ref, points_ref, scale_ref, out_ref):
    mine, wide = env_ref.shape[0], points_ref.shape[0]
    scale = scale_ref[...]
    high = scale.astype(BF16).astype(F32)
    middle = (scale - high).astype(BF16).astype(F32)
    low = scale - high - middle
    row = iota((16, wide), 0)
    parts = jnp.where(row == 0, high, jnp.where(row == 1, middle, jnp.where(row == 2, low, 0.0)))
    for peer in range(out_ref.shape[0]):
        at = slice(peer * LANES, (peer + 1) * LANES)
        out_ref[peer, 0:mine] = env_ref[:, at]
        out_ref[peer, mine : mine + wide] = points_ref[:, at]
        out_ref[peer, mine + wide :] = parts.astype(BF16)


def pack_kernel(env_ref, equation_ref, out_ref, owners, eqs):
    owner, structure = equation_ref[...] // eqs, equation_ref[...] % eqs
    envs = owner.shape[1]
    matches = iota((owners, envs), 0) == owner
    earlier = (iota((envs, envs), 0) < iota((envs, envs), 1)) & (
        iota((envs, envs), 0) // HALF == iota((envs, envs), 1) // HALF
    )
    before = dot(one_hot(matches), one_hot(earlier))
    within = jnp.sum(jnp.where(matches, before, 0.0), axis=0, keepdims=True).astype(jnp.int32)
    place = (iota((1, envs), 1) // HALF) * CAP + within
    slot = owner * GROUP + place
    chosen = one_hot(iota((owners * GROUP, envs), 0) == slot)
    data = dot(chosen, env_ref[:, 0 : envs // env_ref.shape[0]].reshape(envs, LANES))
    named = jnp.where(matches, structure, 0).astype(F32).astype(BF16)
    at = one_hot(iota((LANES, envs), 0) == place)
    labels = dot(named, at, ((1,), (1,)))
    spread = one_hot(iota((owners * GROUP, owners), 0) == iota((owners * GROUP, owners), 1) * GROUP + SLOTS)
    out_ref[...] = (data + dot(spread, labels.astype(BF16))).astype(BF16)


def unpack_kernel(got_ref, panel_ref, out_ref, label_ref):
    rows = got_ref.shape[0]
    sources = rows // GROUP
    slots = sources * SLOTS
    got = got_ref[...]
    slot, row = iota((slots, rows), 0), iota((slots, rows), 1)
    source, place = slot // SLOTS, slot % SLOTS
    data = dot(one_hot(row == source * GROUP + place), got).astype(BF16)
    for copy in range(out_ref.shape[0]):
        out_ref[copy, 0:slots] = data
        out_ref[copy, slots:] = panel_ref[...]
    source, row = iota((sources, rows), 0), iota((sources, rows), 1)
    label_ref[...] = dot(one_hot(row == source * GROUP + SLOTS), got).astype(BF16)


def equations_kernel(
    core_ref,
    own_ref,
    other_ref,
    label_ref,
    points_ref,
    scale_ref,
    panel_ref,
    matrix_ref,
    sums_ref,
    env_ref,
):
    chips, rows, _ = own_ref.shape
    slots = rows - WIDE
    cols = points_ref.shape[0]
    eqs = scale_ref.shape[1] - cols
    core = core_ref[0]
    for chip in range(chips):
        at = pl.multiple_of((2 * chip + core) * LANES, LANES)
        env_ref[:, pl.ds(at, LANES)] = own_ref[chip]
        at = pl.multiple_of((2 * chip + 1 - core) * LANES, LANES)
        env_ref[:, pl.ds(at, LANES)] = other_ref[chip]
    dot_scale = env_ref.shape[1] ** (-0.5)
    sources = label_ref.shape[0]
    source = one_hot(iota((slots, sources), 0) // SLOTS == iota((slots, sources), 1))
    named = dot(source, label_ref[...])
    mine = iota((slots, LANES), 1) == iota((slots, LANES), 0) % SLOTS
    label = jnp.sum(jnp.where(mine, named, 0.0), axis=1, keepdims=True)
    chosen = one_hot(label.astype(jnp.int32) == iota((slots, eqs), 1))
    diagonal = jnp.where(iota((eqs, eqs), 0) == iota((eqs, eqs), 1), scale_ref[:, cols:], 0.0)
    weight = jnp.sum(diagonal, axis=1, keepdims=True)

    def block(points, scale):
        z = dot(env_ref[0:slots, :], points, ((1,), (1,))) * dot_scale
        squared = z * z
        kernel = (scale * squared * squared).astype(BF16)
        return dot(chosen, kernel, ((0,), (0,))) * weight

    parts = panel_ref[...].astype(F32)
    panel = block(env_ref[slots:rows, :], parts[0:1] + parts[1:2] + parts[2:3])
    matrix_ref[:, cols : cols + WIDE] = panel
    gram = dot(panel, panel, ((0,), (0,)), HIGHEST)
    high = gram.astype(BF16)
    low = (gram - high.astype(F32)).astype(BF16)
    members, length, _ = sums_ref.shape
    own_rows = length - 2 * WIDE
    for member in range(members):
        sums_ref[member, own_rows : own_rows + WIDE] = high
        sums_ref[member, own_rows + WIDE : length] = low
    step = 256
    for first in range(0, cols, step):
        part = block(points_ref[first : first + step, :], scale_ref[:, first : first + step])
        matrix_ref[:, first : first + step] = part
        cross = dot(panel, part, ((0,), (0,)), HIGHEST).astype(BF16)
        for at in range(0, step, LANES):
            member, start = divmod((first + at) // LANES * WIDE, own_rows)
            sums_ref[member, start : start + WIDE] = cross[:, at : at + LANES]


def exponent(values):
    largest = jnp.max(jnp.max(jnp.abs(values), axis=0, keepdims=True), axis=1, keepdims=True)
    return jnp.floor(jnp.log2(jnp.maximum(largest, 1e-30)))


def exponent_place(shape, which):
    return (iota(shape, 0) % 8 == which) & (iota(shape, 1) == LANES - 1)


def scaled(cross, gram):
    of_cross, of_gram = exponent(cross), exponent(gram)
    gram = gram * jnp.exp2(TOP - of_gram)
    gram = jnp.where(exponent_place(gram.shape, 0), of_cross, gram)
    gram = jnp.where(exponent_place(gram.shape, 1), of_gram, gram)
    return cross * jnp.exp2(TOP - of_cross), gram


def unscaled_cross(ref, at, own):
    return ref[at, 0:own] * jnp.exp2(ref[at, own : own + 1, LANES - 1 : LANES] - TOP)


def unscaled_gram(ref, at, own):
    return ref[at, own:] * jnp.exp2(ref[at, own + 1 : own + 2, LANES - 1 : LANES] - TOP)


def near_kernel(got_ref, out_ref):
    total = jnp.sum(got_ref[...].astype(F32), axis=0)
    count, length, _ = out_ref.shape
    own_rows = total.shape[0] - 2 * WIDE
    own = own_rows // count
    gram = total[own_rows : own_rows + WIDE] + total[own_rows + WIDE :]
    cross, gram = scaled(total[:own_rows], gram)
    out_ref[:, 0:own] = cross.reshape(count, own, LANES)
    out_ref[:, own:length] = gram.reshape(count, length - own, LANES)


def far_kernel(got_ref, out_ref):
    own = out_ref.shape[0] - 8
    cross = unscaled_cross(got_ref, 0, own)
    gram = unscaled_gram(got_ref, 0, own)
    for source in range(1, got_ref.shape[0]):
        cross = cross + unscaled_cross(got_ref, source, own)
        gram = gram + unscaled_gram(got_ref, source, own)
    taken = exponent_place(gram.shape, 0) | exponent_place(gram.shape, 1)
    cross, gram = scaled(cross, jnp.where(taken, 0.0, gram))
    out_ref[0:own] = cross
    out_ref[own:] = gram


def spread_kernel(column_ref, out_ref):
    own = out_ref.shape[2]
    for at in range(column_ref.shape[0]):
        cross = unscaled_cross(column_ref, at, own)
        for copy in range(out_ref.shape[0]):
            out_ref[copy, at] = cross


def eliminated(gram, shift):
    own = iota((PW, PW), 0) == iota((PW, PW), 1)
    eye = own.astype(F32)
    work = jnp.concatenate([gram + shift * eye, eye], axis=1)
    rows = iota((PW, 1), 0)
    for k in range(0, PW, STEP):
        cols = [jnp.broadcast_to(work[:, k + j : k + j + 1], (PW, WIDE)) for j in range(STEP)]
        pivot = [work[k + i : k + i + 1, :] for i in range(STEP)]
        inner = [[cols[j][k + i : k + i + 1, :] for j in range(STEP)] for i in range(STEP)]
        for a in range(STEP):
            inverse = 1.0 / inner[a][a]
            for i in range(a + 1, STEP):
                ratio = inner[i][a] * inverse
                pivot[i] = pivot[i] - ratio * pivot[a]
                for j in range(a + 1, STEP):
                    inner[i][j] = inner[i][j] - ratio * inner[a][j]
            cols[a] = cols[a] * inverse
            for j in range(a + 1, STEP):
                cols[j] = cols[j] - cols[a] * inner[a][j]
        below = work
        for a in range(STEP):
            below = below - cols[a] * pivot[a]
        work = jnp.where(rows >= k + STEP, below, work)
        for a in range(STEP):
            work = jnp.where(rows == k + a, pivot[a], work)
    pivots = jnp.sum(jnp.where(own, work[:, :PW], 0.0), axis=1, keepdims=True)
    work = work * lax.rsqrt(pivots)
    upper = jnp.where(iota((PW, PW), 0) <= iota((PW, PW), 1), work[:, :PW], 0.0)
    return upper, work[:, PW:]


def factor_kernel(gram_ref, ridge_ref, terms_ref, turn_ref, upper_ref):
    ridge = ridge_ref[0]
    count, length, _ = gram_ref.shape
    held = length - WIDE // count
    gram = jnp.concatenate([unscaled_gram(gram_ref, at, held) for at in range(count)], axis=0)
    taken = exponent_place(gram.shape, 0) | exponent_place(gram.shape, 1)
    gram = jnp.where(taken, gram.T, gram)
    own = iota((PW, PW), 0) == iota((PW, PW), 1)

    def shift_of(a):
        return ridge * jnp.sum(jnp.where(own, a, 0.0)) / PW + 1e-06

    g00, g01, g11 = gram[:PW, :PW], gram[:PW, PW:], gram[PW:, PW:]
    shift0 = shift_of(g00)
    upper0, inverse0 = eliminated(g00, shift0)
    c01 = dot(inverse0, g01, precision=HIGHEST)
    w01 = dot(inverse0, c01, ((0,), (0,)), HIGHEST)
    gram1 = (
        g11
        - dot(c01, c01, ((0,), (0,)), HIGHEST)
        - shift0 * dot(w01, w01, ((0,), (0,)), HIGHEST)
    )
    upper1, inverse1 = eliminated(gram1, shift_of(gram1))
    mixed = c01 + shift0 * dot(inverse0, w01, precision=HIGHEST)
    both = jnp.concatenate([mixed, c01], axis=1)
    taken = dot(both, inverse0, ((0,), (0,)), HIGHEST)
    zero = jnp.zeros((PW, PW), F32)
    terms_ref[0:PW, :] = jnp.concatenate([inverse0, zero], axis=1)
    terms_ref[PW:WIDE, :] = jnp.concatenate(
        [-dot(inverse1, taken[:PW], precision=HIGHEST), inverse1], axis=1
    )
    turn_ref[0:PW, :] = jnp.concatenate([inverse0, zero], axis=1)
    turn_ref[PW:WIDE, :] = jnp.concatenate(
        [-dot(inverse1, taken[PW:], precision=HIGHEST), inverse1], axis=1
    )
    upper_ref[0:PW, :] = jnp.concatenate([upper0, c01], axis=1)
    upper_ref[PW:WIDE, :] = jnp.concatenate([zero, upper1], axis=1)


def final_kernel(
    first_ref, total_ref, terms_ref, turn_ref, upper_ref, matrix_ref, r_ref, reduced_ref, norm_scale
):
    first = first_ref[0] == 0
    cols = reduced_ref.shape[1]
    terms = terms_ref[...]
    q = dot(matrix_ref[:, cols : cols + WIDE], turn_ref[...], ((1,), (1,)), HIGHEST)
    step = 256
    for k in range(cols // step):
        at = slice(k * step, (k + 1) * step)
        cross = jnp.concatenate(
            [
                total_ref[8 * j : 8 * j + 8].reshape(WIDE, LANES)
                for j in range(k * step // LANES, (k + 1) * step // LANES)
            ],
            axis=1,
        )
        coupled = dot(terms, cross, precision=HIGHEST)
        r_ref[:, at] = coupled * norm_scale
        reduced_ref[:, at] = matrix_ref[:, at] - dot(q, coupled, precision=HIGHEST)

    @pl.when(first)
    def _():
        r_ref[:, 0:WIDE] = upper_ref[...] * norm_scale
        reduced_ref[:, 0:WIDE] = q


def body(
    descriptors, sparse_points, point_scale, env_owner, env_structure, row_weight, ridge_factor
):
    owners, peers = lax.axis_size("rows"), lax.axis_size("cols")
    eqs, cols = row_weight.shape[0], point_scale.shape[0]
    mine = descriptors.shape[0]
    envs = mine * peers
    z_groups = [[y * Z + z for z in range(Z)] for y in range(Y)]
    y_groups = [[y * Z + z for y in range(Y)] for z in range(Z)]

    length = mine + WIDE + 16
    sent = pl.pallas_call(
        first_kernel,
        out_shape=jax.ShapeDtypeStruct((peers, length, LANES), BF16),
        grid=(1,),
        in_specs=[
            pl.BlockSpec((mine, peers * LANES), lambda i: (0, 0)),
            pl.BlockSpec((WIDE, peers * LANES), lambda i: (0, 0)),
            pl.BlockSpec((1, WIDE), lambda i: (0, 0)),
        ],
        out_specs=pl.BlockSpec((peers, length, LANES), lambda i: (0, 0, 0)),
        compiler_params=pltpu.CompilerParams(vmem_limit_bytes=60 * 2**20),
    )(descriptors, sparse_points, point_scale.reshape(1, cols))
    got = lax.all_to_all(sent, "cols", split_axis=0, concat_axis=0, tiled=True)
    panel_part, parts = got[0, mine : mine + WIDE], got[0, mine + WIDE :]

    packed = called(
        functools.partial(pack_kernel, owners=owners, eqs=eqs),
        jax.ShapeDtypeStruct((owners * GROUP, LANES), BF16),
        got,
        (env_owner[:, 0] * eqs + env_structure).reshape(1, envs),
    )
    col = lax.axis_index("cols")
    arrived = lax.all_to_all(packed, "rows", split_axis=0, concat_axis=0, tiled=True)
    slots = owners * SLOTS
    slot_rows, labels = called(
        unpack_kernel,
        (
            jax.ShapeDtypeStruct((peers // 2, slots + WIDE, LANES), BF16),
            jax.ShapeDtypeStruct((owners, LANES), BF16),
        ),
        arrived,
        panel_part,
    )
    own = lax.all_to_all(
        slot_rows,
        "cols",
        split_axis=0,
        concat_axis=0,
        tiled=True,
        axis_index_groups=[list(range(0, peers, 2)), list(range(1, peers, 2))],
    )
    other = lax.ppermute(own, "cols", [(c, c ^ 1) for c in range(peers)])

    vmem, smem = pl.BlockSpec(memory_space=pltpu.VMEM), pl.BlockSpec(memory_space=pltpu.SMEM)
    params = pltpu.CompilerParams(vmem_limit_bytes=VMEM_LIMIT)
    own_rows = cols // LANES * WIDE // Y
    matrix, sums = pl.pallas_call(
        equations_kernel,
        out_shape=(
            jax.ShapeDtypeStruct((eqs, cols + WIDE), F32),
            jax.ShapeDtypeStruct((Y, own_rows + 2 * WIDE, LANES), BF16),
        ),
        in_specs=[smem] + [vmem] * 6,
        out_specs=(vmem, vmem),
        scratch_shapes=[pltpu.VMEM((slots + WIDE, peers * LANES), BF16)],
        compiler_params=params,
    )(
        (col % 2).reshape(1),
        own,
        other,
        labels,
        sparse_points,
        jnp.concatenate([point_scale, row_weight]).reshape(1, cols + eqs),
        parts,
    )
    def exchanged(array, groups):
        return lax.all_to_all(
            array, "rows", split_axis=0, concat_axis=0, tiled=True, axis_index_groups=groups
        )

    own = own_rows // Z
    length = own + WIDE // Z
    message = jax.ShapeDtypeStruct((Z, length, LANES), F32)
    summed = called(near_kernel, message, exchanged(sums, y_groups))
    parts = exchanged(summed.astype(F16), z_groups).astype(F32)
    summed = called(far_kernel, jax.ShapeDtypeStruct((length, LANES), F32), parts)
    column = to_each(summed.astype(F16), "rows", z_groups).astype(F32)
    copies = called(spread_kernel, jax.ShapeDtypeStruct((Y, Z, own, LANES), F32), column)
    total = exchanged(copies, y_groups)
    total = total.reshape(owners, own, LANES)

    square = jax.ShapeDtypeStruct((WIDE, WIDE), F32)
    terms, turn, upper = pl.pallas_call(
        factor_kernel,
        out_shape=(square, square, square),
        in_specs=[vmem, smem],
        out_specs=(vmem, vmem, vmem),
        compiler_params=params,
        cost_estimate=pl.CostEstimate(flops=8_000_000_000, bytes_accessed=262144, transcendentals=0),
    )(column, ridge_factor)
    return pl.pallas_call(
        functools.partial(final_kernel, norm_scale=1.0 / math.sqrt(owners * eqs)),
        out_shape=(
            jax.ShapeDtypeStruct((WIDE, cols), F32),
            jax.ShapeDtypeStruct((eqs, cols), F32),
        ),
        in_specs=[smem] + [vmem] * 5,
        out_specs=(vmem, vmem),
        compiler_params=params,
    )(col.reshape(1), total, terms, turn, upper, matrix)


def solution(mesh):
    return jax.shard_map(
        body,
        mesh=mesh,
        in_specs=(
            P(("rows", "cols"), None),
            P("cols", None),
            P("cols"),
            P("rows", None),
            P("rows"),
            P("rows"),
            P(),
        ),
        out_specs=(P(None, "cols"), P("rows", "cols")),
        check_vma=False,
    )
```

```python
import functools
import math

import jax
import jax.numpy as jnp
from jax import lax
from jax.experimental import pallas as pl
from jax.experimental.pallas import tpu as pltpu
from jax.sharding import PartitionSpec as P

PW = 64
PANELS = 2
WIDE = PW * PANELS
CAP = 3
HALF = 128
LANES = 128
GROUP = 8
SLOTS = 2 * CAP
STEP = 4
Y, Z = 4, 16
F32, BF16, F16 = jnp.float32, jnp.bfloat16, jnp.float16
TOP = 14
HIGHEST = lax.Precision.HIGHEST
VMEM_LIMIT = 20 * 2**20


def dot(a, b, dims=((1,), (0,)), precision=None):
    return lax.dot_general(
        a, b, (dims, ((), ())), precision=precision, preferred_element_type=F32
    )


def halves(a):
    high = a.astype(BF16)
    return high, (a - high.astype(F32)).astype(BF16)


def dot3(a, b):
    (ah, al), (bh, bl) = a, b
    return dot(ah, bh) + (dot(ah, bl) + dot(al, bh))


def iota(shape, dim):
    return lax.broadcasted_iota(jnp.int32, shape, dim)


def one_hot(condition):
    return condition.astype(F32).astype(BF16)


def called(kernel, out_shape, *args):
    return pl.pallas_call(
        kernel,
        out_shape=out_shape,
        compiler_params=pltpu.CompilerParams(vmem_limit_bytes=VMEM_LIMIT),
    )(*args)


def to_each(array, axis, groups=None):
    count = lax.axis_size(axis) if groups is None else len(groups[0])
    copies = jnp.broadcast_to(array, (count, *array.shape))
    return lax.all_to_all(
        copies, axis, split_axis=0, concat_axis=0, tiled=True, axis_index_groups=groups
    )


def first_kernel(env_ref, points_ref, scale_ref, out_ref):
    mine, wide = env_ref.shape[0], points_ref.shape[0]
    scale = scale_ref[...]
    high = scale.astype(BF16).astype(F32)
    middle = (scale - high).astype(BF16).astype(F32)
    low = scale - high - middle
    row = iota((16, wide), 0)
    parts = jnp.where(row == 0, high, jnp.where(row == 1, middle, jnp.where(row == 2, low, 0.0)))
    for peer in range(out_ref.shape[0]):
        at = slice(peer * LANES, (peer + 1) * LANES)
        out_ref[peer, 0:mine] = env_ref[:, at]
        out_ref[peer, mine : mine + wide] = points_ref[:, at]
        out_ref[peer, mine + wide :] = parts.astype(BF16)


def pack_kernel(env_ref, equation_ref, out_ref, owners, eqs):
    owner, structure = equation_ref[...] // eqs, equation_ref[...] % eqs
    envs = owner.shape[1]
    matches = iota((owners, envs), 0) == owner
    earlier = (iota((envs, envs), 0) < iota((envs, envs), 1)) & (
        iota((envs, envs), 0) // HALF == iota((envs, envs), 1) // HALF
    )
    before = dot(one_hot(matches), one_hot(earlier))
    within = jnp.sum(jnp.where(matches, before, 0.0), axis=0, keepdims=True).astype(jnp.int32)
    place = (iota((1, envs), 1) // HALF) * CAP + within
    slot = owner * GROUP + place
    chosen = one_hot(iota((owners * GROUP, envs), 0) == slot)
    data = dot(chosen, env_ref[:, 0 : envs // env_ref.shape[0]].reshape(envs, LANES))
    named = jnp.where(matches, structure, 0).astype(F32).astype(BF16)
    at = one_hot(iota((LANES, envs), 0) == place)
    labels = dot(named, at, ((1,), (1,)))
    spread = one_hot(iota((owners * GROUP, owners), 0) == iota((owners * GROUP, owners), 1) * GROUP + SLOTS)
    out_ref[...] = (data + dot(spread, labels.astype(BF16))).astype(BF16)


def unpack_kernel(got_ref, panel_ref, out_ref, label_ref):
    rows = got_ref.shape[0]
    sources = rows // GROUP
    slots = sources * SLOTS
    got = got_ref[...]
    slot, row = iota((slots, rows), 0), iota((slots, rows), 1)
    source, place = slot // SLOTS, slot % SLOTS
    data = dot(one_hot(row == source * GROUP + place), got).astype(BF16)
    for copy in range(out_ref.shape[0]):
        out_ref[copy, 0:slots] = data
        out_ref[copy, slots:] = panel_ref[...]
    source, row = iota((sources, rows), 0), iota((sources, rows), 1)
    label_ref[...] = dot(one_hot(row == source * GROUP + SLOTS), got).astype(BF16)


def equations_kernel(
    core_ref,
    own_ref,
    other_ref,
    label_ref,
    points_ref,
    scale_ref,
    panel_ref,
    matrix_ref,
    sums_ref,
    env_ref,
):
    chips, rows, _ = own_ref.shape
    slots = rows - WIDE
    cols = points_ref.shape[0]
    eqs = scale_ref.shape[1] - cols
    core = core_ref[0]
    for chip in range(chips):
        at = pl.multiple_of((2 * chip + core) * LANES, LANES)
        env_ref[:, pl.ds(at, LANES)] = own_ref[chip]
        at = pl.multiple_of((2 * chip + 1 - core) * LANES, LANES)
        env_ref[:, pl.ds(at, LANES)] = other_ref[chip]
    dot_scale = env_ref.shape[1] ** (-0.5)
    sources = label_ref.shape[0]
    source = one_hot(iota((slots, sources), 0) // SLOTS == iota((slots, sources), 1))
    named = dot(source, label_ref[...])
    mine = iota((slots, LANES), 1) == iota((slots, LANES), 0) % SLOTS
    label = jnp.sum(jnp.where(mine, named, 0.0), axis=1, keepdims=True)
    chosen = (label.astype(jnp.int32) == iota((slots, eqs), 1)).astype(F32).T.astype(BF16)
    diagonal = jnp.where(iota((eqs, eqs), 0) == iota((eqs, eqs), 1), scale_ref[:, cols:], 0.0)
    weight = jnp.sum(diagonal, axis=1, keepdims=True)

    def block(points, scale):
        z = dot(env_ref[0:slots, :], points, ((1,), (1,))) * dot_scale
        squared = z * z
        kernel = (scale * squared * squared).astype(BF16)
        return dot(chosen, kernel) * weight

    parts = panel_ref[...].astype(F32)
    panel = block(env_ref[slots:rows, :], parts[0:1] + parts[1:2] + parts[2:3])
    matrix_ref[:, cols : cols + WIDE] = panel
    turned = panel.T
    gram = dot(turned, panel, precision=HIGHEST)
    high, low = halves(gram[:PW])
    last_high, last_low = halves(gram[PW:, PW:])
    rest = jnp.concatenate([high, low, jnp.concatenate([last_high, last_low], axis=1)], axis=0)
    members, length, _ = sums_ref.shape
    own_rows = length - 3 * PW
    for member in range(members):
        sums_ref[member, own_rows:length] = rest
    turned = turned.astype(BF16)
    step = 256
    for first in range(0, cols, step):
        part = block(points_ref[first : first + step, :], scale_ref[:, first : first + step])
        matrix_ref[:, first : first + step] = part
        cross = dot(turned, part.astype(BF16)).astype(BF16)
        for at in range(0, step, LANES):
            member, start = divmod((first + at) // LANES * WIDE, own_rows)
            sums_ref[member, start : start + WIDE] = cross[:, at : at + LANES]


def exponent(values):
    largest = jnp.max(jnp.max(jnp.abs(values), axis=0, keepdims=True), axis=1, keepdims=True)
    return jnp.floor(jnp.log2(jnp.maximum(largest, 1e-30)))


def exponent_place(shape, which):
    return (iota(shape, 0) % 8 == which) & (iota(shape, 1) == LANES - 1)


def scaled(cross, gram):
    of_cross, of_gram = exponent(cross), exponent(gram)
    gram = gram * jnp.exp2(TOP - of_gram)
    gram = jnp.where(exponent_place(gram.shape, 0), of_cross, gram)
    gram = jnp.where(exponent_place(gram.shape, 1), of_gram, gram)
    return cross * jnp.exp2(TOP - of_cross), gram


def unscaled_cross(ref, at, own):
    return ref[at, 0:own] * jnp.exp2(ref[at, own : own + 1, LANES - 1 : LANES] - TOP)


def unscaled_gram(ref, at, own):
    return ref[at, own:] * jnp.exp2(ref[at, own + 1 : own + 2, LANES - 1 : LANES] - TOP)


def near_kernel(got_ref, out_ref):
    total = jnp.sum(got_ref[...].astype(F32), axis=0)
    count, length, _ = out_ref.shape
    own_rows = total.shape[0] - 3 * PW
    own = own_rows // count
    upper = total[own_rows : own_rows + PW] + total[own_rows + PW : own_rows + 2 * PW]
    last = total[own_rows + 2 * PW :]
    last = last[:, :PW] + last[:, PW:]
    lower = jnp.concatenate([upper.T[PW:], last], axis=1)
    gram = jnp.concatenate([upper, lower], axis=0)
    cross, gram = scaled(total[:own_rows], gram)
    out_ref[:, 0:own] = cross.reshape(count, own, LANES)
    out_ref[:, own:length] = gram.reshape(count, length - own, LANES)


def far_kernel(got_ref, out_ref):
    own = out_ref.shape[0] - 8
    cross = unscaled_cross(got_ref, 0, own)
    gram = unscaled_gram(got_ref, 0, own)
    for source in range(1, got_ref.shape[0]):
        cross = cross + unscaled_cross(got_ref, source, own)
        gram = gram + unscaled_gram(got_ref, source, own)
    taken = exponent_place(gram.shape, 0) | exponent_place(gram.shape, 1)
    cross, gram = scaled(cross, jnp.where(taken, 0.0, gram))
    out_ref[0:own] = cross
    out_ref[own:] = gram


def spread_kernel(column_ref, out_ref):
    own = out_ref.shape[2]
    for at in range(column_ref.shape[0]):
        cross = unscaled_cross(column_ref, at, own)
        for copy in range(out_ref.shape[0]):
            out_ref[copy, at] = cross


def eliminated(gram, shift):
    own = iota((PW, PW), 0) == iota((PW, PW), 1)
    eye = own.astype(F32)
    work = jnp.concatenate([gram + shift * eye, eye], axis=1)
    rows = iota((PW, 1), 0)
    for k in range(0, PW, STEP):
        cols = [jnp.broadcast_to(work[:, k + j : k + j + 1], (PW, WIDE)) for j in range(STEP)]
        pivot = [work[k + i : k + i + 1, :] for i in range(STEP)]
        inner = [[cols[j][k + i : k + i + 1, :] for j in range(STEP)] for i in range(STEP)]
        for a in range(STEP):
            inverse = 1.0 / inner[a][a]
            for i in range(a + 1, STEP):
                ratio = inner[i][a] * inverse
                pivot[i] = pivot[i] - ratio * pivot[a]
                for j in range(a + 1, STEP):
                    inner[i][j] = inner[i][j] - ratio * inner[a][j]
            cols[a] = cols[a] * inverse
            for j in range(a + 1, STEP):
                cols[j] = cols[j] - cols[a] * inner[a][j]
        below = work
        for a in range(STEP):
            below = below - cols[a] * pivot[a]
        work = jnp.where(rows >= k + STEP, below, work)
        for a in range(STEP):
            work = jnp.where(rows == k + a, pivot[a], work)
    pivots = jnp.sum(jnp.where(own, work[:, :PW], 0.0), axis=1, keepdims=True)
    work = work * lax.rsqrt(pivots)
    upper = jnp.where(iota((PW, PW), 0) <= iota((PW, PW), 1), work[:, :PW], 0.0)
    return upper, work[:, PW:]


def factor_kernel(gram_ref, ridge_ref, terms_ref, turn_ref, upper_ref):
    ridge = ridge_ref[0]
    count, length, _ = gram_ref.shape
    held = length - WIDE // count
    gram = jnp.concatenate([unscaled_gram(gram_ref, at, held) for at in range(count)], axis=0)
    taken = exponent_place(gram.shape, 0) | exponent_place(gram.shape, 1)
    gram = jnp.where(taken, gram.T, gram)
    own = iota((PW, PW), 0) == iota((PW, PW), 1)

    def shift_of(a):
        return ridge * jnp.sum(jnp.where(own, a, 0.0)) / PW + 1e-06

    g00, g01, g11 = gram[:PW, :PW], gram[:PW, PW:], gram[PW:, PW:]
    shift0 = shift_of(g00)
    upper0, inverse0 = eliminated(g00, shift0)
    c01 = dot(inverse0, g01, precision=HIGHEST)
    w01 = dot(inverse0, c01, ((0,), (0,)), HIGHEST)
    gram1 = (
        g11
        - dot(c01, c01, ((0,), (0,)), HIGHEST)
        - shift0 * dot(w01, w01, ((0,), (0,)), HIGHEST)
    )
    upper1, inverse1 = eliminated(gram1, shift_of(gram1))
    mixed = c01 + shift0 * dot(inverse0, w01, precision=HIGHEST)
    both = jnp.concatenate([mixed, c01], axis=1)
    taken = dot(both, inverse0, ((0,), (0,)), HIGHEST)
    zero = jnp.zeros((PW, PW), F32)
    terms_ref[0:PW, :] = jnp.concatenate([inverse0, zero], axis=1)
    terms_ref[PW:WIDE, :] = jnp.concatenate(
        [-dot(inverse1, taken[:PW], precision=HIGHEST), inverse1], axis=1
    )
    turn_ref[0:PW, :] = jnp.concatenate([inverse0, zero], axis=1)
    turn_ref[PW:WIDE, :] = jnp.concatenate(
        [-dot(inverse1, taken[PW:], precision=HIGHEST), inverse1], axis=1
    )
    upper_ref[0:PW, :] = jnp.concatenate([upper0, c01], axis=1)
    upper_ref[PW:WIDE, :] = jnp.concatenate([zero, upper1], axis=1)


def final_kernel(
    first_ref, total_ref, terms_ref, turn_ref, upper_ref, matrix_ref, r_ref, reduced_ref, norm_scale
):
    first = first_ref[0] == 0
    cols = reduced_ref.shape[1]
    terms = halves(terms_ref[...])
    q = dot(matrix_ref[:, cols : cols + WIDE], turn_ref[...], ((1,), (1,)), HIGHEST)
    q_parts = halves(q)
    step = 256
    for k in range(cols // step):
        at = slice(k * step, (k + 1) * step)
        cross = jnp.concatenate(
            [
                total_ref[8 * j : 8 * j + 8].reshape(WIDE, LANES)
                for j in range(k * step // LANES, (k + 1) * step // LANES)
            ],
            axis=1,
        )
        coupled = dot3(terms, halves(cross))
        r_ref[:, at] = coupled * norm_scale
        reduced_ref[:, at] = matrix_ref[:, at] - dot3(q_parts, halves(coupled))

    @pl.when(first)
    def _():
        r_ref[:, 0:WIDE] = upper_ref[...] * norm_scale
        reduced_ref[:, 0:WIDE] = q


def body(
    descriptors, sparse_points, point_scale, env_owner, env_structure, row_weight, ridge_factor
):
    owners, peers = lax.axis_size("rows"), lax.axis_size("cols")
    eqs, cols = row_weight.shape[0], point_scale.shape[0]
    mine = descriptors.shape[0]
    envs = mine * peers
    z_groups = [[y * Z + z for z in range(Z)] for y in range(Y)]
    y_groups = [[y * Z + z for y in range(Y)] for z in range(Z)]

    length = mine + WIDE + 16
    sent = pl.pallas_call(
        first_kernel,
        out_shape=jax.ShapeDtypeStruct((peers, length, LANES), BF16),
        grid=(1,),
        in_specs=[
            pl.BlockSpec((mine, peers * LANES), lambda i: (0, 0)),
            pl.BlockSpec((WIDE, peers * LANES), lambda i: (0, 0)),
            pl.BlockSpec((1, WIDE), lambda i: (0, 0)),
        ],
        out_specs=pl.BlockSpec((peers, length, LANES), lambda i: (0, 0, 0)),
        compiler_params=pltpu.CompilerParams(vmem_limit_bytes=60 * 2**20),
    )(descriptors, sparse_points, point_scale.reshape(1, cols))
    got = lax.all_to_all(sent, "cols", split_axis=0, concat_axis=0, tiled=True)
    panel_part, parts = got[0, mine : mine + WIDE], got[0, mine + WIDE :]

    packed = called(
        functools.partial(pack_kernel, owners=owners, eqs=eqs),
        jax.ShapeDtypeStruct((owners * GROUP, LANES), BF16),
        got,
        (env_owner[:, 0] * eqs + env_structure).reshape(1, envs),
    )
    col = lax.axis_index("cols")
    arrived = lax.all_to_all(packed, "rows", split_axis=0, concat_axis=0, tiled=True)
    slots = owners * SLOTS
    slot_rows, labels = called(
        unpack_kernel,
        (
            jax.ShapeDtypeStruct((peers // 2, slots + WIDE, LANES), BF16),
            jax.ShapeDtypeStruct((owners, LANES), BF16),
        ),
        arrived,
        panel_part,
    )
    own = lax.all_to_all(
        slot_rows,
        "cols",
        split_axis=0,
        concat_axis=0,
        tiled=True,
        axis_index_groups=[list(range(0, peers, 2)), list(range(1, peers, 2))],
    )
    other = lax.ppermute(own, "cols", [(c, c ^ 1) for c in range(peers)])

    vmem, smem = pl.BlockSpec(memory_space=pltpu.VMEM), pl.BlockSpec(memory_space=pltpu.SMEM)
    params = pltpu.CompilerParams(vmem_limit_bytes=VMEM_LIMIT)
    own_rows = cols // LANES * WIDE // Y
    matrix, sums = pl.pallas_call(
        equations_kernel,
        out_shape=(
            jax.ShapeDtypeStruct((eqs, cols + WIDE), F32),
            jax.ShapeDtypeStruct((Y, own_rows + 3 * PW, LANES), BF16),
        ),
        in_specs=[smem] + [vmem] * 6,
        out_specs=(vmem, vmem),
        scratch_shapes=[pltpu.VMEM((slots + WIDE, peers * LANES), BF16)],
        compiler_params=params,
    )(
        (col % 2).reshape(1),
        own,
        other,
        labels,
        sparse_points,
        jnp.concatenate([point_scale, row_weight]).reshape(1, cols + eqs),
        parts,
    )
    def exchanged(array, groups):
        return lax.all_to_all(
            array, "rows", split_axis=0, concat_axis=0, tiled=True, axis_index_groups=groups
        )

    own = own_rows // Z
    length = own + WIDE // Z
    message = jax.ShapeDtypeStruct((Z, length, LANES), F32)
    summed = called(near_kernel, message, exchanged(sums, y_groups))
    parts = exchanged(summed.astype(F16), z_groups).astype(F32)
    summed = called(far_kernel, jax.ShapeDtypeStruct((length, LANES), F32), parts)
    column = to_each(summed.astype(F16), "rows", z_groups).astype(F32)
    copies = called(spread_kernel, jax.ShapeDtypeStruct((Y, Z, own, LANES), F32), column)
    total = exchanged(copies, y_groups)
    total = total.reshape(owners, own, LANES)

    square = jax.ShapeDtypeStruct((WIDE, WIDE), F32)
    terms, turn, upper = pl.pallas_call(
        factor_kernel,
        out_shape=(square, square, square),
        in_specs=[vmem, smem],
        out_specs=(vmem, vmem, vmem),
        compiler_params=params,
        cost_estimate=pl.CostEstimate(flops=8_000_000_000, bytes_accessed=262144, transcendentals=0),
    )(column, ridge_factor)
    return pl.pallas_call(
        functools.partial(final_kernel, norm_scale=1.0 / math.sqrt(owners * eqs)),
        out_shape=(
            jax.ShapeDtypeStruct((WIDE, cols), F32),
            jax.ShapeDtypeStruct((eqs, cols), F32),
        ),
        in_specs=[smem] + [vmem] * 5,
        out_specs=(vmem, vmem),
        compiler_params=params,
    )(col.reshape(1), total, terms, turn, upper, matrix)


def solution(mesh):
    return jax.shard_map(
        body,
        mesh=mesh,
        in_specs=(
            P(("rows", "cols"), None),
            P("cols", None),
            P("cols"),
            P("rows", None),
            P("rows"),
            P("rows"),
            P(),
        ),
        out_specs=(P(None, "cols"), P("rows", "cols")),
        check_vma=False,
    )
```

```python
import functools
import math

import jax
import jax.numpy as jnp
from jax import lax
from jax.experimental import pallas as pl
from jax.experimental.pallas import tpu as pltpu
from jax.sharding import PartitionSpec as P

PW = 64
PANELS = 2
WIDE = PW * PANELS
CAP = 3
HALF = 128
LANES = 128
GROUP = 8
SLOTS = 2 * CAP
STEP = 4
Y, Z = 4, 16
F32, BF16, F16 = jnp.float32, jnp.bfloat16, jnp.float16
TOP = 14
HIGHEST = lax.Precision.HIGHEST
VMEM_LIMIT = 20 * 2**20


def dot(a, b, dims=((1,), (0,)), precision=None):
    return lax.dot_general(
        a, b, (dims, ((), ())), precision=precision, preferred_element_type=F32
    )


def halves(a):
    high = a.astype(BF16)
    return high, (a - high.astype(F32)).astype(BF16)


def dot3(a, b):
    (ah, al), (bh, bl) = a, b
    return dot(ah, bh) + (dot(ah, bl) + dot(al, bh))


def iota(shape, dim):
    return lax.broadcasted_iota(jnp.int32, shape, dim)


def one_hot(condition):
    return condition.astype(F32).astype(BF16)


def called(kernel, out_shape, *args):
    return pl.pallas_call(
        kernel,
        out_shape=out_shape,
        compiler_params=pltpu.CompilerParams(vmem_limit_bytes=VMEM_LIMIT),
    )(*args)


def to_each(array, axis, groups=None):
    count = lax.axis_size(axis) if groups is None else len(groups[0])
    copies = jnp.broadcast_to(array, (count, *array.shape))
    return lax.all_to_all(
        copies, axis, split_axis=0, concat_axis=0, tiled=True, axis_index_groups=groups
    )


def first_kernel(env_ref, points_ref, scale_ref, out_ref):
    mine, wide = env_ref.shape[0], points_ref.shape[0]
    scale = scale_ref[...]
    high = scale.astype(BF16).astype(F32)
    middle = (scale - high).astype(BF16).astype(F32)
    low = scale - high - middle
    row = iota((16, wide), 0)
    parts = jnp.where(row == 0, high, jnp.where(row == 1, middle, jnp.where(row == 2, low, 0.0)))
    for peer in range(out_ref.shape[0]):
        at = slice(peer * LANES, (peer + 1) * LANES)
        out_ref[peer, 0:mine] = env_ref[:, at]
        out_ref[peer, mine : mine + wide] = points_ref[:, at]
        out_ref[peer, mine + wide :] = parts.astype(BF16)


def pack_kernel(env_ref, equation_ref, out_ref, owners, eqs):
    owner, structure = equation_ref[...] // eqs, equation_ref[...] % eqs
    envs = owner.shape[1]
    matches = iota((owners, envs), 0) == owner
    earlier = (iota((envs, envs), 0) < iota((envs, envs), 1)) & (
        iota((envs, envs), 0) // HALF == iota((envs, envs), 1) // HALF
    )
    before = dot(one_hot(matches), one_hot(earlier))
    within = jnp.sum(jnp.where(matches, before, 0.0), axis=0, keepdims=True).astype(jnp.int32)
    place = (iota((1, envs), 1) // HALF) * CAP + within
    slot = owner * GROUP + place
    chosen = one_hot(iota((owners * GROUP, envs), 0) == slot)
    data = dot(chosen, env_ref[:, 0 : envs // env_ref.shape[0]].reshape(envs, LANES))
    named = jnp.where(matches, structure, 0).astype(F32).astype(BF16)
    at = one_hot(iota((LANES, envs), 0) == place)
    labels = dot(named, at, ((1,), (1,)))
    spread = one_hot(iota((owners * GROUP, owners), 0) == iota((owners * GROUP, owners), 1) * GROUP + SLOTS)
    out_ref[...] = (data + dot(spread, labels.astype(BF16))).astype(BF16)


def unpack_kernel(got_ref, panel_ref, out_ref, label_ref):
    rows = got_ref.shape[0]
    sources = rows // GROUP
    slots = sources * SLOTS
    got = got_ref[...]
    slot, row = iota((slots, rows), 0), iota((slots, rows), 1)
    source, place = slot // SLOTS, slot % SLOTS
    data = dot(one_hot(row == source * GROUP + place), got).astype(BF16)
    for copy in range(out_ref.shape[0]):
        out_ref[copy, 0:slots] = data
        out_ref[copy, slots:] = panel_ref[...]
    source, row = iota((sources, rows), 0), iota((sources, rows), 1)
    label_ref[...] = dot(one_hot(row == source * GROUP + SLOTS), got).astype(BF16)


def equations_kernel(
    core_ref,
    own_ref,
    other_ref,
    label_ref,
    points_ref,
    scale_ref,
    panel_ref,
    matrix_ref,
    sums_ref,
    env_ref,
):
    chips, rows, _ = own_ref.shape
    slots = rows - WIDE
    cols = points_ref.shape[0]
    eqs = scale_ref.shape[1] - cols
    core = core_ref[0]
    for chip in range(chips):
        at = pl.multiple_of((2 * chip + core) * LANES, LANES)
        env_ref[:, pl.ds(at, LANES)] = own_ref[chip]
        at = pl.multiple_of((2 * chip + 1 - core) * LANES, LANES)
        env_ref[:, pl.ds(at, LANES)] = other_ref[chip]
    dot_scale = env_ref.shape[1] ** (-0.5)
    sources = label_ref.shape[0]
    source = one_hot(iota((slots, sources), 0) // SLOTS == iota((slots, sources), 1))
    named = dot(source, label_ref[...])
    mine = iota((slots, LANES), 1) == iota((slots, LANES), 0) % SLOTS
    label = jnp.sum(jnp.where(mine, named, 0.0), axis=1, keepdims=True)
    chosen = (label.astype(jnp.int32) == iota((slots, eqs), 1)).astype(F32).T.astype(BF16)
    diagonal = jnp.where(iota((eqs, eqs), 0) == iota((eqs, eqs), 1), scale_ref[:, cols:], 0.0)
    weight = jnp.sum(diagonal, axis=1, keepdims=True)

    def block(points, scale):
        z = dot(env_ref[0:slots, :], points, ((1,), (1,))) * dot_scale
        squared = z * z
        kernel = (scale * squared * squared).astype(BF16)
        return dot(chosen, kernel) * weight

    parts = panel_ref[...].astype(F32)
    panel = block(env_ref[slots:rows, :], parts[0:1] + parts[1:2] + parts[2:3])
    matrix_ref[:, cols : cols + WIDE] = panel
    turned = panel.T
    gram = dot(turned, panel, precision=HIGHEST)
    high, low = halves(gram[:PW])
    last_high, last_low = halves(gram[PW:, PW:])
    rest = jnp.concatenate([high, low, jnp.concatenate([last_high, last_low], axis=1)], axis=0)
    members, length, _ = sums_ref.shape
    own_rows = length - 3 * PW
    for member in range(members):
        sums_ref[member, own_rows:length] = rest
    turned = turned.astype(BF16)
    step = 256
    for first in range(0, cols, step):
        part = block(points_ref[first : first + step, :], scale_ref[:, first : first + step])
        matrix_ref[:, first : first + step] = part
        cross = dot(turned, part.astype(BF16)).astype(BF16)
        for at in range(0, step, LANES):
            member, start = divmod((first + at) // LANES * WIDE, own_rows)
            sums_ref[member, start : start + WIDE] = cross[:, at : at + LANES]


def exponent(values):
    largest = jnp.max(jnp.max(jnp.abs(values), axis=0, keepdims=True), axis=1, keepdims=True)
    return jnp.floor(jnp.log2(jnp.maximum(largest, 1e-30)))


def exponent_place(shape, which):
    return (iota(shape, 0) % 8 == which) & (iota(shape, 1) == LANES - 1)


def scaled(cross, gram):
    of_cross, of_gram = exponent(cross), exponent(gram)
    gram = gram * jnp.exp2(TOP - of_gram)
    gram = jnp.where(exponent_place(gram.shape, 0), of_cross, gram)
    gram = jnp.where(exponent_place(gram.shape, 1), of_gram, gram)
    return cross * jnp.exp2(TOP - of_cross), gram


def unscaled_cross(ref, at, own):
    return ref[at, 0:own] * jnp.exp2(ref[at, own : own + 1, LANES - 1 : LANES] - TOP)


def unscaled_gram(ref, at, own):
    return ref[at, own:] * jnp.exp2(ref[at, own + 1 : own + 2, LANES - 1 : LANES] - TOP)


def near_kernel(got_ref, out_ref):
    total = jnp.sum(got_ref[...].astype(F32), axis=0)
    count, length, _ = out_ref.shape
    own_rows = total.shape[0] - 3 * PW
    own = own_rows // count
    upper = total[own_rows : own_rows + PW] + total[own_rows + PW : own_rows + 2 * PW]
    last = total[own_rows + 2 * PW :]
    last = last[:, :PW] + last[:, PW:]
    lower = jnp.concatenate([upper.T[PW:], last], axis=1)
    gram = jnp.concatenate([upper, lower], axis=0)
    cross, gram = scaled(total[:own_rows], gram)
    out_ref[:, 0:own] = cross.reshape(count, own, LANES)
    out_ref[:, own:length] = gram.reshape(count, length - own, LANES)


def far_kernel(got_ref, out_ref):
    own = out_ref.shape[0] - 8
    cross = unscaled_cross(got_ref, 0, own)
    gram = unscaled_gram(got_ref, 0, own)
    for source in range(1, got_ref.shape[0]):
        cross = cross + unscaled_cross(got_ref, source, own)
        gram = gram + unscaled_gram(got_ref, source, own)
    taken = exponent_place(gram.shape, 0) | exponent_place(gram.shape, 1)
    cross, gram = scaled(cross, jnp.where(taken, 0.0, gram))
    out_ref[0:own] = cross
    out_ref[own:] = gram


def eliminated(gram, shift):
    own = iota((PW, PW), 0) == iota((PW, PW), 1)
    eye = own.astype(F32)
    work = jnp.concatenate([gram + shift * eye, eye], axis=1)
    rows = iota((PW, 1), 0)
    for k in range(0, PW, STEP):
        cols = [jnp.broadcast_to(work[:, k + j : k + j + 1], (PW, WIDE)) for j in range(STEP)]
        pivot = [work[k + i : k + i + 1, :] for i in range(STEP)]
        inner = [[cols[j][k + i : k + i + 1, :] for j in range(STEP)] for i in range(STEP)]
        for a in range(STEP):
            inverse = 1.0 / inner[a][a]
            for i in range(a + 1, STEP):
                ratio = inner[i][a] * inverse
                pivot[i] = pivot[i] - ratio * pivot[a]
                for j in range(a + 1, STEP):
                    inner[i][j] = inner[i][j] - ratio * inner[a][j]
            cols[a] = cols[a] * inverse
            for j in range(a + 1, STEP):
                cols[j] = cols[j] - cols[a] * inner[a][j]
        below = work
        for a in range(STEP):
            below = below - cols[a] * pivot[a]
        work = jnp.where(rows >= k + STEP, below, work)
        for a in range(STEP):
            work = jnp.where(rows == k + a, pivot[a], work)
    pivots = jnp.sum(jnp.where(own, work[:, :PW], 0.0), axis=1, keepdims=True)
    work = work * lax.rsqrt(pivots)
    upper = jnp.where(iota((PW, PW), 0) <= iota((PW, PW), 1), work[:, :PW], 0.0)
    return upper, work[:, PW:]


def factor_kernel(gram_ref, ridge_ref, terms_ref, turn_ref, upper_ref):
    ridge = ridge_ref[0]
    count, length, _ = gram_ref.shape
    held = length - WIDE // count
    gram = jnp.concatenate([unscaled_gram(gram_ref, at, held) for at in range(count)], axis=0)
    taken = exponent_place(gram.shape, 0) | exponent_place(gram.shape, 1)
    gram = jnp.where(taken, gram.T, gram)
    own = iota((PW, PW), 0) == iota((PW, PW), 1)

    def shift_of(a):
        return ridge * jnp.sum(jnp.where(own, a, 0.0)) / PW + 1e-06

    g00, g01, g11 = gram[:PW, :PW], gram[:PW, PW:], gram[PW:, PW:]
    shift0 = shift_of(g00)
    upper0, inverse0 = eliminated(g00, shift0)
    c01 = dot(inverse0, g01, precision=HIGHEST)
    w01 = dot(inverse0, c01, ((0,), (0,)), HIGHEST)
    gram1 = (
        g11
        - dot(c01, c01, ((0,), (0,)), HIGHEST)
        - shift0 * dot(w01, w01, ((0,), (0,)), HIGHEST)
    )
    upper1, inverse1 = eliminated(gram1, shift_of(gram1))
    mixed = c01 + shift0 * dot(inverse0, w01, precision=HIGHEST)
    both = jnp.concatenate([mixed, c01], axis=1)
    taken = dot(both, inverse0, ((0,), (0,)), HIGHEST)
    zero = jnp.zeros((PW, PW), F32)
    terms_ref[0:PW, :] = jnp.concatenate([inverse0, zero], axis=1)
    terms_ref[PW:WIDE, :] = jnp.concatenate(
        [-dot(inverse1, taken[:PW], precision=HIGHEST), inverse1], axis=1
    )
    turn_ref[0:PW, :] = jnp.concatenate([inverse0, zero], axis=1)
    turn_ref[PW:WIDE, :] = jnp.concatenate(
        [-dot(inverse1, taken[PW:], precision=HIGHEST), inverse1], axis=1
    )
    upper_ref[0:PW, :] = jnp.concatenate([upper0, c01], axis=1)
    upper_ref[PW:WIDE, :] = jnp.concatenate([zero, upper1], axis=1)


def final_kernel(
    first_ref, total_ref, terms_ref, turn_ref, upper_ref, matrix_ref, r_ref, reduced_ref, norm_scale
):
    first = first_ref[0] == 0
    cols = reduced_ref.shape[1]
    own = WIDE // 8
    terms = halves(terms_ref[...])
    q = dot(matrix_ref[:, cols : cols + WIDE], turn_ref[...], ((1,), (1,)), HIGHEST)
    q_parts = halves(q)
    step = 256
    for k in range(cols // step):
        at = slice(k * step, (k + 1) * step)
        cross = jnp.concatenate(
            [
                jnp.concatenate(
                    [unscaled_cross(total_ref, at, own) for at in range(8 * j, 8 * j + 8)], axis=0
                )
                for j in range(k * step // LANES, (k + 1) * step // LANES)
            ],
            axis=1,
        )
        coupled = dot3(terms, halves(cross))
        r_ref[:, at] = coupled * norm_scale
        reduced_ref[:, at] = matrix_ref[:, at] - dot3(q_parts, halves(coupled))

    @pl.when(first)
    def _():
        r_ref[:, 0:WIDE] = upper_ref[...] * norm_scale
        reduced_ref[:, 0:WIDE] = q


def body(
    descriptors, sparse_points, point_scale, env_owner, env_structure, row_weight, ridge_factor
):
    owners, peers = lax.axis_size("rows"), lax.axis_size("cols")
    eqs, cols = row_weight.shape[0], point_scale.shape[0]
    mine = descriptors.shape[0]
    envs = mine * peers
    z_groups = [[y * Z + z for z in range(Z)] for y in range(Y)]
    y_groups = [[y * Z + z for y in range(Y)] for z in range(Z)]

    length = mine + WIDE + 16
    sent = pl.pallas_call(
        first_kernel,
        out_shape=jax.ShapeDtypeStruct((peers, length, LANES), BF16),
        grid=(1,),
        in_specs=[
            pl.BlockSpec((mine, peers * LANES), lambda i: (0, 0)),
            pl.BlockSpec((WIDE, peers * LANES), lambda i: (0, 0)),
            pl.BlockSpec((1, WIDE), lambda i: (0, 0)),
        ],
        out_specs=pl.BlockSpec((peers, length, LANES), lambda i: (0, 0, 0)),
        compiler_params=pltpu.CompilerParams(vmem_limit_bytes=60 * 2**20),
    )(descriptors, sparse_points, point_scale.reshape(1, cols))
    got = lax.all_to_all(sent, "cols", split_axis=0, concat_axis=0, tiled=True)
    panel_part, parts = got[0, mine : mine + WIDE], got[0, mine + WIDE :]

    packed = called(
        functools.partial(pack_kernel, owners=owners, eqs=eqs),
        jax.ShapeDtypeStruct((owners * GROUP, LANES), BF16),
        got,
        (env_owner[:, 0] * eqs + env_structure).reshape(1, envs),
    )
    col = lax.axis_index("cols")
    arrived = lax.all_to_all(packed, "rows", split_axis=0, concat_axis=0, tiled=True)
    slots = owners * SLOTS
    slot_rows, labels = called(
        unpack_kernel,
        (
            jax.ShapeDtypeStruct((peers // 2, slots + WIDE, LANES), BF16),
            jax.ShapeDtypeStruct((owners, LANES), BF16),
        ),
        arrived,
        panel_part,
    )
    own = lax.all_to_all(
        slot_rows,
        "cols",
        split_axis=0,
        concat_axis=0,
        tiled=True,
        axis_index_groups=[list(range(0, peers, 2)), list(range(1, peers, 2))],
    )
    other = lax.ppermute(own, "cols", [(c, c ^ 1) for c in range(peers)])

    vmem, smem = pl.BlockSpec(memory_space=pltpu.VMEM), pl.BlockSpec(memory_space=pltpu.SMEM)
    params = pltpu.CompilerParams(vmem_limit_bytes=VMEM_LIMIT)
    own_rows = cols // LANES * WIDE // Y
    matrix, sums = pl.pallas_call(
        equations_kernel,
        out_shape=(
            jax.ShapeDtypeStruct((eqs, cols + WIDE), F32),
            jax.ShapeDtypeStruct((Y, own_rows + 3 * PW, LANES), BF16),
        ),
        in_specs=[smem] + [vmem] * 6,
        out_specs=(vmem, vmem),
        scratch_shapes=[pltpu.VMEM((slots + WIDE, peers * LANES), BF16)],
        compiler_params=params,
    )(
        (col % 2).reshape(1),
        own,
        other,
        labels,
        sparse_points,
        jnp.concatenate([point_scale, row_weight]).reshape(1, cols + eqs),
        parts,
    )
    def exchanged(array, groups):
        return lax.all_to_all(
            array, "rows", split_axis=0, concat_axis=0, tiled=True, axis_index_groups=groups
        )

    own = own_rows // Z
    length = own + WIDE // Z
    message = jax.ShapeDtypeStruct((Z, length, LANES), F32)
    summed = called(near_kernel, message, exchanged(sums, y_groups))
    parts = exchanged(summed.astype(F16), z_groups).astype(F32)
    summed = called(far_kernel, jax.ShapeDtypeStruct((length, LANES), F32), parts)
    column = to_each(summed.astype(F16), "rows", z_groups)
    total = to_each(column, "rows", y_groups).reshape(owners, length, LANES).astype(F32)

    square = jax.ShapeDtypeStruct((WIDE, WIDE), F32)
    terms, turn, upper = pl.pallas_call(
        factor_kernel,
        out_shape=(square, square, square),
        in_specs=[vmem, smem],
        out_specs=(vmem, vmem, vmem),
        compiler_params=params,
        cost_estimate=pl.CostEstimate(flops=8_000_000_000, bytes_accessed=262144, transcendentals=0),
    )(column.astype(F32), ridge_factor)
    return pl.pallas_call(
        functools.partial(final_kernel, norm_scale=1.0 / math.sqrt(owners * eqs)),
        out_shape=(
            jax.ShapeDtypeStruct((WIDE, cols), F32),
            jax.ShapeDtypeStruct((eqs, cols), F32),
        ),
        in_specs=[smem] + [vmem] * 5,
        out_specs=(vmem, vmem),
        compiler_params=params,
    )(col.reshape(1), total, terms, turn, upper, matrix)


def solution(mesh):
    return jax.shard_map(
        body,
        mesh=mesh,
        in_specs=(
            P(("rows", "cols"), None),
            P("cols", None),
            P("cols"),
            P("rows", None),
            P("rows"),
            P("rows"),
            P(),
        ),
        out_specs=(P(None, "cols"), P("rows", "cols")),
        check_vma=False,
    )
```

```python
import functools
import math

import jax
import jax.numpy as jnp
from jax import lax
from jax.experimental import pallas as pl
from jax.experimental.pallas import tpu as pltpu
from jax.sharding import PartitionSpec as P

PW = 64
PANELS = 2
WIDE = PW * PANELS
CAP = 3
HALF = 128
LANES = 128
GROUP = 8
SLOTS = 2 * CAP
STEP = 4
Y, Z = 4, 16
F32, BF16, F16 = jnp.float32, jnp.bfloat16, jnp.float16
TOP = 14
HIGHEST = lax.Precision.HIGHEST
VMEM_LIMIT = 20 * 2**20


def dot(a, b, dims=((1,), (0,)), precision=None):
    return lax.dot_general(
        a, b, (dims, ((), ())), precision=precision, preferred_element_type=F32
    )


def halves(a):
    high = a.astype(BF16)
    return high, (a - high.astype(F32)).astype(BF16)


def dot3(a, b):
    (ah, al), (bh, bl) = a, b
    return dot(ah, bh) + (dot(ah, bl) + dot(al, bh))


def iota(shape, dim):
    return lax.broadcasted_iota(jnp.int32, shape, dim)


def one_hot(condition):
    return condition.astype(F32).astype(BF16)


def called(kernel, out_shape, *args):
    return pl.pallas_call(
        kernel,
        out_shape=out_shape,
        compiler_params=pltpu.CompilerParams(vmem_limit_bytes=VMEM_LIMIT),
    )(*args)


def to_each(array, axis, groups=None):
    count = lax.axis_size(axis) if groups is None else len(groups[0])
    copies = jnp.broadcast_to(array, (count, *array.shape))
    return lax.all_to_all(
        copies, axis, split_axis=0, concat_axis=0, tiled=True, axis_index_groups=groups
    )


def first_kernel(env_ref, points_ref, scale_ref, out_ref):
    mine, wide = env_ref.shape[0], points_ref.shape[0]
    scale = scale_ref[...]
    high = scale.astype(BF16).astype(F32)
    middle = (scale - high).astype(BF16).astype(F32)
    low = scale - high - middle
    row = iota((16, wide), 0)
    parts = jnp.where(row == 0, high, jnp.where(row == 1, middle, jnp.where(row == 2, low, 0.0)))
    for peer in range(out_ref.shape[0]):
        at = slice(peer * LANES, (peer + 1) * LANES)
        out_ref[peer, 0:mine] = env_ref[:, at]
        out_ref[peer, mine : mine + wide] = points_ref[:, at]
        out_ref[peer, mine + wide :] = parts.astype(BF16)


def pack_kernel(env_ref, equation_ref, out_ref, owners, eqs):
    owner, structure = equation_ref[...] // eqs, equation_ref[...] % eqs
    envs = owner.shape[1]
    matches = iota((owners, envs), 0) == owner
    earlier = (iota((envs, envs), 0) < iota((envs, envs), 1)) & (
        iota((envs, envs), 0) // HALF == iota((envs, envs), 1) // HALF
    )
    before = dot(one_hot(matches), one_hot(earlier))
    within = jnp.sum(jnp.where(matches, before, 0.0), axis=0, keepdims=True).astype(jnp.int32)
    place = (iota((1, envs), 1) // HALF) * CAP + within
    slot = owner * GROUP + place
    chosen = one_hot(iota((owners * GROUP, envs), 0) == slot)
    data = dot(chosen, env_ref[:, 0 : envs // env_ref.shape[0]].reshape(envs, LANES))
    named = jnp.where(matches, structure, 0).astype(F32).astype(BF16)
    at = one_hot(iota((LANES, envs), 0) == place)
    labels = dot(named, at, ((1,), (1,)))
    spread = one_hot(iota((owners * GROUP, owners), 0) == iota((owners * GROUP, owners), 1) * GROUP + SLOTS)
    out_ref[...] = (data + dot(spread, labels.astype(BF16))).astype(BF16)


def unpack_kernel(got_ref, panel_ref, out_ref, label_ref):
    rows = got_ref.shape[0]
    sources = rows // GROUP
    slots = sources * SLOTS
    got = got_ref[...]
    slot, row = iota((slots, rows), 0), iota((slots, rows), 1)
    source, place = slot // SLOTS, slot % SLOTS
    data = dot(one_hot(row == source * GROUP + place), got).astype(BF16)
    for copy in range(out_ref.shape[0]):
        out_ref[copy, 0:slots] = data
        out_ref[copy, slots:] = panel_ref[...]
    source, row = iota((sources, rows), 0), iota((sources, rows), 1)
    label_ref[...] = dot(one_hot(row == source * GROUP + SLOTS), got).astype(BF16)


def equations_kernel(
    core_ref,
    own_ref,
    other_ref,
    label_ref,
    points_ref,
    scale_ref,
    panel_ref,
    matrix_ref,
    sums_ref,
    env_ref,
):
    chips, rows, _ = own_ref.shape
    slots = rows - WIDE
    cols = points_ref.shape[1]
    eqs = scale_ref.shape[1] - cols
    core = core_ref[0]
    for chip in range(chips):
        at = pl.multiple_of((2 * chip + core) * LANES, LANES)
        env_ref[:, pl.ds(at, LANES)] = own_ref[chip]
        at = pl.multiple_of((2 * chip + 1 - core) * LANES, LANES)
        env_ref[:, pl.ds(at, LANES)] = other_ref[chip]
    dot_scale = env_ref.shape[1] ** (-0.5)
    sources = label_ref.shape[0]
    source = one_hot(iota((slots, sources), 0) // SLOTS == iota((slots, sources), 1))
    named = dot(source, label_ref[...])
    mine = iota((slots, LANES), 1) == iota((slots, LANES), 0) % SLOTS
    label = jnp.sum(jnp.where(mine, named, 0.0), axis=1, keepdims=True)
    chosen = (label.astype(jnp.int32) == iota((slots, eqs), 1)).astype(F32).T.astype(BF16)
    diagonal = jnp.where(iota((eqs, eqs), 0) == iota((eqs, eqs), 1), scale_ref[:, cols:], 0.0)
    weight = jnp.sum(diagonal, axis=1, keepdims=True)

    def block(points, scale):
        z = dot(env_ref[0:slots, :], points) * dot_scale
        squared = z * z
        kernel = (scale * squared * squared).astype(BF16)
        return dot(chosen, kernel) * weight

    parts = panel_ref[...].astype(F32)
    panel = block(env_ref[slots:rows, :].T, parts[0:1] + parts[1:2] + parts[2:3])
    matrix_ref[:, cols : cols + WIDE] = panel
    turned = panel.T
    gram = dot(turned, panel, precision=HIGHEST)
    high, low = halves(gram[:PW])
    last_high, last_low = halves(gram[PW:, PW:])
    rest = jnp.concatenate([high, low, jnp.concatenate([last_high, last_low], axis=1)], axis=0)
    members, length, _ = sums_ref.shape
    own_rows = length - 3 * PW
    for member in range(members):
        sums_ref[member, own_rows:length] = rest
    turned = turned.astype(BF16)
    step = 256
    for first in range(0, cols, step):
        part = block(points_ref[:, first : first + step], scale_ref[:, first : first + step])
        matrix_ref[:, first : first + step] = part
        cross = dot(turned, part.astype(BF16)).astype(BF16)
        for at in range(0, step, LANES):
            member, start = divmod((first + at) // LANES * WIDE, own_rows)
            sums_ref[member, start : start + WIDE] = cross[:, at : at + LANES]


def exponent(values):
    largest = jnp.max(jnp.max(jnp.abs(values), axis=0, keepdims=True), axis=1, keepdims=True)
    return jnp.floor(jnp.log2(jnp.maximum(largest, 1e-30)))


def exponent_place(shape, which):
    return (iota(shape, 0) % 8 == which) & (iota(shape, 1) == LANES - 1)


def scaled(cross, gram):
    of_cross, of_gram = exponent(cross), exponent(gram)
    gram = gram * jnp.exp2(TOP - of_gram)
    gram = jnp.where(exponent_place(gram.shape, 0), of_cross, gram)
    gram = jnp.where(exponent_place(gram.shape, 1), of_gram, gram)
    return cross * jnp.exp2(TOP - of_cross), gram


def unscaled_cross(ref, at, own):
    return ref[at, 0:own] * jnp.exp2(ref[at, own : own + 1, LANES - 1 : LANES] - TOP)


def unscaled_gram(ref, at, own):
    return ref[at, own:] * jnp.exp2(ref[at, own + 1 : own + 2, LANES - 1 : LANES] - TOP)


def near_kernel(got_ref, out_ref):
    total = jnp.sum(got_ref[...].astype(F32), axis=0)
    count, length, _ = out_ref.shape
    own_rows = total.shape[0] - 3 * PW
    own = own_rows // count
    upper = total[own_rows : own_rows + PW] + total[own_rows + PW : own_rows + 2 * PW]
    last = total[own_rows + 2 * PW :]
    last = last[:, :PW] + last[:, PW:]
    lower = jnp.concatenate([upper.T[PW:], last], axis=1)
    gram = jnp.concatenate([upper, lower], axis=0)
    cross, gram = scaled(total[:own_rows], gram)
    out_ref[:, 0:own] = cross.reshape(count, own, LANES)
    out_ref[:, own:length] = gram.reshape(count, length - own, LANES)


def far_kernel(got_ref, out_ref):
    own = out_ref.shape[0] - 8
    cross = unscaled_cross(got_ref, 0, own)
    gram = unscaled_gram(got_ref, 0, own)
    for source in range(1, got_ref.shape[0]):
        cross = cross + unscaled_cross(got_ref, source, own)
        gram = gram + unscaled_gram(got_ref, source, own)
    taken = exponent_place(gram.shape, 0) | exponent_place(gram.shape, 1)
    cross, gram = scaled(cross, jnp.where(taken, 0.0, gram))
    out_ref[0:own] = cross
    out_ref[own:] = gram


def eliminated(gram, shift):
    own = iota((PW, PW), 0) == iota((PW, PW), 1)
    eye = own.astype(F32)
    work = jnp.concatenate([gram + shift * eye, eye], axis=1)
    rows = iota((PW, 1), 0)
    for k in range(0, PW, STEP):
        cols = [jnp.broadcast_to(work[:, k + j : k + j + 1], (PW, WIDE)) for j in range(STEP)]
        pivot = [work[k + i : k + i + 1, :] for i in range(STEP)]
        inner = [[cols[j][k + i : k + i + 1, :] for j in range(STEP)] for i in range(STEP)]
        for a in range(STEP):
            inverse = 1.0 / inner[a][a]
            for i in range(a + 1, STEP):
                ratio = inner[i][a] * inverse
                pivot[i] = pivot[i] - ratio * pivot[a]
                for j in range(a + 1, STEP):
                    inner[i][j] = inner[i][j] - ratio * inner[a][j]
            cols[a] = cols[a] * inverse
            for j in range(a + 1, STEP):
                cols[j] = cols[j] - cols[a] * inner[a][j]
        below = work
        for a in range(STEP):
            below = below - cols[a] * pivot[a]
        work = jnp.where(rows >= k + STEP, below, work)
        for a in range(STEP):
            work = jnp.where(rows == k + a, pivot[a], work)
    pivots = jnp.sum(jnp.where(own, work[:, :PW], 0.0), axis=1, keepdims=True)
    work = work * lax.rsqrt(pivots)
    upper = jnp.where(iota((PW, PW), 0) <= iota((PW, PW), 1), work[:, :PW], 0.0)
    return upper, work[:, PW:]


def factor_kernel(gram_ref, ridge_ref, terms_ref, turn_ref, upper_ref):
    ridge = ridge_ref[0]
    count, length, _ = gram_ref.shape
    held = length - WIDE // count
    gram = jnp.concatenate([unscaled_gram(gram_ref, at, held) for at in range(count)], axis=0)
    taken = exponent_place(gram.shape, 0) | exponent_place(gram.shape, 1)
    gram = jnp.where(taken, gram.T, gram)
    own = iota((PW, PW), 0) == iota((PW, PW), 1)

    def shift_of(a):
        return ridge * jnp.sum(jnp.where(own, a, 0.0)) / PW + 1e-06

    g00, g01, g11 = gram[:PW, :PW], gram[:PW, PW:], gram[PW:, PW:]
    shift0 = shift_of(g00)
    upper0, inverse0 = eliminated(g00, shift0)
    c01 = dot(inverse0, g01, precision=HIGHEST)
    w01 = dot(inverse0, c01, ((0,), (0,)), HIGHEST)
    gram1 = (
        g11
        - dot(c01, c01, ((0,), (0,)), HIGHEST)
        - shift0 * dot(w01, w01, ((0,), (0,)), HIGHEST)
    )
    upper1, inverse1 = eliminated(gram1, shift_of(gram1))
    mixed = c01 + shift0 * dot(inverse0, w01, precision=HIGHEST)
    both = jnp.concatenate([mixed, c01], axis=1)
    taken = dot(both, inverse0, ((0,), (0,)), HIGHEST)
    zero = jnp.zeros((PW, PW), F32)
    terms_ref[0:PW, :] = jnp.concatenate([inverse0, zero], axis=1)
    terms_ref[PW:WIDE, :] = jnp.concatenate(
        [-dot(inverse1, taken[:PW], precision=HIGHEST), inverse1], axis=1
    )
    turn_ref[0:PW, :] = jnp.concatenate([inverse0, zero], axis=1)
    turn_ref[PW:WIDE, :] = jnp.concatenate(
        [-dot(inverse1, taken[PW:], precision=HIGHEST), inverse1], axis=1
    )
    upper_ref[0:PW, :] = jnp.concatenate([upper0, c01], axis=1)
    upper_ref[PW:WIDE, :] = jnp.concatenate([zero, upper1], axis=1)


def final_kernel(
    first_ref, total_ref, terms_ref, turn_ref, upper_ref, matrix_ref, r_ref, reduced_ref, norm_scale
):
    first = first_ref[0] == 0
    cols = reduced_ref.shape[1]
    own = WIDE // 8
    terms = halves(terms_ref[...])
    q = dot(matrix_ref[:, cols : cols + WIDE], turn_ref[...], ((1,), (1,)), HIGHEST)
    q_parts = halves(q)
    step = 256
    for k in range(cols // step):
        at = slice(k * step, (k + 1) * step)
        cross = jnp.concatenate(
            [
                jnp.concatenate(
                    [unscaled_cross(total_ref, at, own) for at in range(8 * j, 8 * j + 8)], axis=0
                )
                for j in range(k * step // LANES, (k + 1) * step // LANES)
            ],
            axis=1,
        )
        coupled = dot3(terms, halves(cross))
        r_ref[:, at] = coupled * norm_scale
        reduced_ref[:, at] = matrix_ref[:, at] - dot3(q_parts, halves(coupled))

    @pl.when(first)
    def _():
        r_ref[:, 0:WIDE] = upper_ref[...] * norm_scale
        reduced_ref[:, 0:WIDE] = q


def body(
    descriptors, sparse_points, point_scale, env_owner, env_structure, row_weight, ridge_factor
):
    owners, peers = lax.axis_size("rows"), lax.axis_size("cols")
    eqs, cols = row_weight.shape[0], point_scale.shape[0]
    mine = descriptors.shape[0]
    envs = mine * peers
    z_groups = [[y * Z + z for z in range(Z)] for y in range(Y)]
    y_groups = [[y * Z + z for y in range(Y)] for z in range(Z)]

    length = mine + WIDE + 16
    sent = pl.pallas_call(
        first_kernel,
        out_shape=jax.ShapeDtypeStruct((peers, length, LANES), BF16),
        grid=(1,),
        in_specs=[
            pl.BlockSpec((mine, peers * LANES), lambda i: (0, 0)),
            pl.BlockSpec((WIDE, peers * LANES), lambda i: (0, 0)),
            pl.BlockSpec((1, WIDE), lambda i: (0, 0)),
        ],
        out_specs=pl.BlockSpec((peers, length, LANES), lambda i: (0, 0, 0)),
        compiler_params=pltpu.CompilerParams(vmem_limit_bytes=60 * 2**20),
    )(descriptors, sparse_points, point_scale.reshape(1, cols))
    got = lax.all_to_all(sent, "cols", split_axis=0, concat_axis=0, tiled=True)
    panel_part, parts = got[0, mine : mine + WIDE], got[0, mine + WIDE :]

    packed = called(
        functools.partial(pack_kernel, owners=owners, eqs=eqs),
        jax.ShapeDtypeStruct((owners * GROUP, LANES), BF16),
        got,
        (env_owner[:, 0] * eqs + env_structure).reshape(1, envs),
    )
    col = lax.axis_index("cols")
    packed, points = lax.optimization_barrier((packed, sparse_points))
    points = points.T
    arrived = lax.all_to_all(packed, "rows", split_axis=0, concat_axis=0, tiled=True)
    arrived, points = lax.optimization_barrier((arrived, points))
    slots = owners * SLOTS
    slot_rows, labels = called(
        unpack_kernel,
        (
            jax.ShapeDtypeStruct((peers // 2, slots + WIDE, LANES), BF16),
            jax.ShapeDtypeStruct((owners, LANES), BF16),
        ),
        arrived,
        panel_part,
    )
    own = lax.all_to_all(
        slot_rows,
        "cols",
        split_axis=0,
        concat_axis=0,
        tiled=True,
        axis_index_groups=[list(range(0, peers, 2)), list(range(1, peers, 2))],
    )
    other = lax.ppermute(own, "cols", [(c, c ^ 1) for c in range(peers)])

    vmem, smem = pl.BlockSpec(memory_space=pltpu.VMEM), pl.BlockSpec(memory_space=pltpu.SMEM)
    params = pltpu.CompilerParams(vmem_limit_bytes=VMEM_LIMIT)
    own_rows = cols // LANES * WIDE // Y
    matrix, sums = pl.pallas_call(
        equations_kernel,
        out_shape=(
            jax.ShapeDtypeStruct((eqs, cols + WIDE), F32),
            jax.ShapeDtypeStruct((Y, own_rows + 3 * PW, LANES), BF16),
        ),
        in_specs=[smem] + [vmem] * 6,
        out_specs=(vmem, vmem),
        scratch_shapes=[pltpu.VMEM((slots + WIDE, peers * LANES), BF16)],
        compiler_params=params,
    )(
        (col % 2).reshape(1),
        own,
        other,
        labels,
        points,
        jnp.concatenate([point_scale, row_weight]).reshape(1, cols + eqs),
        parts,
    )
    def exchanged(array, groups):
        return lax.all_to_all(
            array, "rows", split_axis=0, concat_axis=0, tiled=True, axis_index_groups=groups
        )

    own = own_rows // Z
    length = own + WIDE // Z
    message = jax.ShapeDtypeStruct((Z, length, LANES), F32)
    summed = called(near_kernel, message, exchanged(sums, y_groups))
    parts = exchanged(summed.astype(F16), z_groups).astype(F32)
    summed = called(far_kernel, jax.ShapeDtypeStruct((length, LANES), F32), parts)
    column = to_each(summed.astype(F16), "rows", z_groups)
    total = to_each(column, "rows", y_groups).reshape(owners, length, LANES).astype(F32)

    square = jax.ShapeDtypeStruct((WIDE, WIDE), F32)
    terms, turn, upper = pl.pallas_call(
        factor_kernel,
        out_shape=(square, square, square),
        in_specs=[vmem, smem],
        out_specs=(vmem, vmem, vmem),
        compiler_params=params,
        cost_estimate=pl.CostEstimate(flops=8_000_000_000, bytes_accessed=262144, transcendentals=0),
    )(column.astype(F32), ridge_factor)
    return pl.pallas_call(
        functools.partial(final_kernel, norm_scale=1.0 / math.sqrt(owners * eqs)),
        out_shape=(
            jax.ShapeDtypeStruct((WIDE, cols), F32),
            jax.ShapeDtypeStruct((eqs, cols), F32),
        ),
        in_specs=[smem] + [vmem] * 5,
        out_specs=(vmem, vmem),
        compiler_params=params,
    )(col.reshape(1), total, terms, turn, upper, matrix)


def solution(mesh):
    return jax.shard_map(
        body,
        mesh=mesh,
        in_specs=(
            P(("rows", "cols"), None),
            P("cols", None),
            P("cols"),
            P("rows", None),
            P("rows"),
            P("rows"),
            P(),
        ),
        out_specs=(P(None, "cols"), P("rows", "cols")),
        check_vma=False,
    )
```
